32 devices in a mesh: seq: 8 (over z, x), chan: 4 (over y, core).
Axes of the slice: x: 2, y: 2, z: 4, core: 2. Of those that a mesh axis runs over, the one named last changes fastest.
Arguments:
- tokens: int32 [2048], P('seq'), may hold values from 0 to 255
- embed_table: bfloat16 [256, 2048], P(None, 'chan'), may hold values from -6 to 6
- short_conv: float32 [3, 2048], P(None, 'chan'), may hold values from -4 to 4
- query_branch: bfloat16 [2048, 2048], P('seq', 'chan'), may hold values from -6 to 6
- key_branch: bfloat16 [2048, 2048], P('seq', 'chan'), may hold values from -6 to 6
- decay_rate: float32 [2048], P('chan'), may hold values from 4.8828125e-05 to 0.1, as said below
- weight_first: float32 [33, 64], replicated, may hold values from -1 to 1
- weight_second: float32 [64, 64], replicated, may hold values from -0.75 to 0.75
- weight_third: float32 [64, 2048], P(None, 'chan'), may hold values from -0.75 to 0.75
- skip_gain: float32 [2048], P('chan'), may hold values from -4 to 4
- cotangent: bfloat16 [2048, 2048], P('seq', 'chan'), may hold values from -6 to 6
Outputs:
- operator_out: bfloat16 [2048, 2048], P('seq', 'chan')
- grad_query: bfloat16 [2048, 2048], P('seq', 'chan')
- grad_key: bfloat16 [2048, 2048], P('seq', 'chan')
- grad_embed: float32 [256, 2048], P('seq', 'chan')
- grad_short: float32 [3, 2048], P(None, 'chan')
- grad_skip: float32 [2048], P('chan')
- grad_first: float32 [33, 64], replicated
- grad_second: float32 [64, 64], replicated
- grad_third: float32 [64, 2048], P(None, 'chan')
The draws below stay inside these ranges and needn't reach their ends.
Inputs may be any that keep to these rules, and one draw needn't show every extreme that they name: `decay_rate`: each channel's decay rate is either slow, log-uniform from 0.1 / 2048 to 2 / 2048, or fast, log-uniform from 0.02 to 0.1, clipped to the stated range.
All inputs are finite; a program needn't handle non-finite values.
Results may differ from the reference program's by a relative error of at most 0.0014.
Values sent between devices are 32-bit elements; how exact they have to be, the bound alone decides.
A program may use at most 64 MiB of HBM per device.

```python
import math
import jax
import jax.numpy as jnp
from jax import lax

D = 2048
VOCAB = 256
FH = 64
BANDS = 16
FEAT = 33
SEQLEN = 2048


def draw_decay_rate(key, part):
    pick_key = jax.random.fold_in(key, 11)
    slow_key = jax.random.fold_in(key, 12)
    fast_key = jax.random.fold_in(key, 13)
    slow_share = 0.5
    chosen = jax.random.uniform(pick_key, (D,), jnp.float32) < slow_share
    slow_rate = jnp.exp(jax.random.uniform(slow_key, (D,), jnp.float32, math.log(0.1), math.log(2.0))) / SEQLEN
    fast_rate = jnp.exp(jax.random.uniform(fast_key, (D,), jnp.float32, math.log(0.02), math.log(0.1)))
    return jnp.clip(jnp.where(chosen, slow_rate, fast_rate), 0.1 / SEQLEN, 0.1).astype(jnp.float32)


def with_ends(drawn, rng, smallest, largest):
    place = [jax.random.randint(jax.random.fold_in(rng, axis), (), 0, length) for axis, length in enumerate(drawn.shape)]
    longest = drawn.shape.index(max(drawn.shape))
    beside = place[:longest] + [(place[longest] + 1) % drawn.shape[longest]] + place[longest + 1:]
    return drawn.at[tuple(place)].set(smallest).at[tuple(beside)].set(largest)


def block_scale(rng, extent, cuts, least, largest):
    def one(dim, parts):
        heights = jax.random.uniform(jax.random.fold_in(jax.random.fold_in(rng, 6), dim), (parts,), jnp.float32, least / len(cuts), largest / len(cuts))
        return jnp.repeat(jnp.exp(heights), extent[dim] // parts).reshape((-1,) + (1,) * (len(extent) - dim - 1))

    loudness = one(*cuts[0])
    for cut in cuts[1:]:
        loudness = loudness * one(*cut)
    return loudness


def scatter_about(rng, shape, deviation, most, shards=(), kind=jnp.bfloat16):
    array = deviation * jax.random.normal(rng, shape, jnp.float32)
    if shards:
        array = array * block_scale(rng, shape, shards, -0.22, 0.18)
    return jnp.clip(array, -most, most).astype(kind)


def setup_inputs(seed: int = 0) -> dict:
    splits = jax.random.split(jax.random.key(seed), 12)
    tokens = with_ends(jax.random.randint(splits[0], (SEQLEN,), 0, VOCAB), jax.random.fold_in(splits[0], 1), 0, VOCAB - 1).astype(jnp.int32)
    embed_table = scatter_about(splits[1], (VOCAB, D), 1.0, 6.0, ((1, 4),))
    short_conv = scatter_about(splits[2], (3, D), 0.7, 4.0, ((1, 4),), jnp.float32)
    query_branch = scatter_about(splits[3], (SEQLEN, D), 1.0, 6.0, ((0, 8), (1, 4)))
    key_branch = scatter_about(splits[4], (SEQLEN, D), 1.0, 6.0, ((0, 8), (1, 4)))
    decay_rate = draw_decay_rate(jax.random.fold_in(splits[11], 71), 0)
    weight_first = scatter_about(splits[6], (FEAT, FH), FEAT ** -0.5, 1.0, (), jnp.float32)
    weight_second = scatter_about(splits[7], (FH, FH), FH ** -0.5, 0.75, (), jnp.float32)
    weight_third = scatter_about(splits[8], (FH, D), FH ** -0.5, 0.75, ((1, 4),), jnp.float32)
    skip_gain = scatter_about(splits[9], (D,), 1.0, 4.0, ((0, 4),), jnp.float32)
    cotangent = scatter_about(splits[10], (SEQLEN, D), 1.0, 6.0, ((0, 8), (1, 4)))
    return {"tokens": tokens, "embed_table": embed_table, "short_conv": short_conv, "query_branch": query_branch, "key_branch": key_branch, "decay_rate": decay_rate, "weight_first": weight_first, "weight_second": weight_second, "weight_third": weight_third, "skip_gain": skip_gain, "cotangent": cotangent}


highest = lax.Precision.HIGHEST
two_pi = 2.0 * math.pi

def features(positions, length):
    frequency = 2 ** jnp.arange(BANDS, dtype=jnp.int32) + 1
    phases = positions[:, None] * frequency[None, :] % length
    angles = phases.astype(jnp.float32) * (two_pi / length)
    ramp_col = positions.astype(jnp.float32)[:, None] / length
    return jnp.concatenate([ramp_col, jnp.cos(angles), jnp.sin(angles)], axis=1)

def filter_forward(positions, length, weight_first, weight_second, weight_third, decay_rate):
    embedding = features(positions, length)
    pre_one = jnp.dot(embedding, weight_first, precision=highest, preferred_element_type=jnp.float32)
    act_one = jnp.sin(pre_one)
    pre_two = jnp.dot(act_one, weight_second, precision=highest, preferred_element_type=jnp.float32)
    act_two = jnp.sin(pre_two)
    shaped = jnp.dot(act_two, weight_third, precision=highest, preferred_element_type=jnp.float32)
    scaling = jnp.sqrt(jnp.expm1(-2.0 * decay_rate) / jnp.expm1(-2.0 * length * decay_rate))
    window = scaling[None, :] * jnp.exp(-decay_rate[None, :] * positions.astype(jnp.float32)[:, None])
    return (shaped * window, (window, embedding, pre_one, act_one, pre_two, act_two))

def filter_head(grad_filter, saved_acts, weight_third):
    window, embedding, pre_one, act_one, pre_two, act_two = saved_acts
    grad_shaped = grad_filter * window
    grad_third = jnp.dot(act_two.T, grad_shaped, precision=highest, preferred_element_type=jnp.float32)
    grad_act_two = jnp.dot(grad_shaped, weight_third.T, precision=highest, preferred_element_type=jnp.float32)
    return (grad_third, grad_act_two)

def filter_tail(grad_act_two, saved_acts, weight_second):
    window, embedding, pre_one, act_one, pre_two, act_two = saved_acts
    grad_pre_two = grad_act_two * jnp.cos(pre_two)
    grad_second = jnp.dot(act_one.T, grad_pre_two, precision=highest, preferred_element_type=jnp.float32)
    grad_act_one = jnp.dot(grad_pre_two, weight_second.T, precision=highest, preferred_element_type=jnp.float32)
    grad_pre_one = grad_act_one * jnp.cos(pre_one)
    grad_first = jnp.dot(embedding.T, grad_pre_one, precision=highest, preferred_element_type=jnp.float32)
    return (grad_first, grad_second)

def reference(tokens, embed_table, short_conv, query_branch, key_branch, decay_rate, weight_first, weight_second, weight_third, skip_gain, cotangent):
    length = tokens.shape[0]
    points = 2 * length
    inv_root = 1.0 / math.sqrt(length)
    vocab_size = embed_table.shape[0]
    embedded = embed_table[tokens].astype(jnp.float32)
    padded = jnp.concatenate([jnp.zeros((2, embedded.shape[1]), jnp.float32), embedded], axis=0)
    value_branch = short_conv[0] * padded[2:] + short_conv[1] * padded[1:-1] + short_conv[2] * padded[:-2]
    keyed_value = key_branch.astype(jnp.float32) * value_branch
    query_rows = query_branch.astype(jnp.float32)
    grad_out = cotangent.astype(jnp.float32)
    positions = jnp.arange(length, dtype=jnp.int32)
    filter_rows, saved_acts = filter_forward(positions, length, weight_first, weight_second, weight_third, decay_rate)
    grad_z = grad_out * query_rows
    spec_keyed = jnp.fft.rfft(keyed_value, n=points, axis=0)
    spec_filter = jnp.fft.rfft(filter_rows, n=points, axis=0)
    spec_grad = jnp.fft.rfft(grad_z, n=points, axis=0)
    convolved = jnp.fft.irfft(spec_keyed * spec_filter, n=points, axis=0)[:length]
    back_keyed = jnp.fft.irfft(jnp.conj(spec_filter) * spec_grad, n=points, axis=0)[:length]
    grad_filter = jnp.fft.irfft(jnp.conj(spec_keyed) * spec_grad, n=points, axis=0)[:length]
    inner_sum = convolved + skip_gain * keyed_value
    operator_out = (query_rows * inner_sum).astype(jnp.bfloat16)
    grad_query = (grad_out * inner_sum).astype(jnp.bfloat16)
    grad_keyed = back_keyed + skip_gain * grad_z
    grad_key = (grad_keyed * value_branch).astype(jnp.bfloat16)
    grad_value = grad_keyed * key_branch.astype(jnp.float32)
    grad_short = jnp.stack([lax.optimization_barrier(jnp.sum(grad_value * padded[2 - offset:2 - offset + length], axis=0)) for offset in range(3)]) * inv_root
    grad_skip = lax.optimization_barrier(jnp.sum(grad_z * keyed_value, axis=0)) * inv_root
    grad_embed = jnp.zeros((vocab_size, embedded.shape[1]), jnp.float32)
    for offset in range(3):
        grad_embed = grad_embed + jax.ops.segment_sum(short_conv[offset] * grad_value[offset:], tokens[:length - offset], num_segments=vocab_size)
    grad_embed = grad_embed * inv_root
    grad_third, grad_act_two = filter_head(grad_filter, saved_acts, weight_third)
    grad_first, grad_second = filter_tail(grad_act_two, saved_acts, weight_second)
    return (operator_out, grad_query, grad_key, grad_embed, grad_short, grad_skip, grad_first * inv_root, grad_second * inv_root, grad_third * inv_root)
```

```python
import functools
import math

import jax
import jax.numpy as jnp
import ml_dtypes
import numpy as np
from jax import lax
from jax.experimental import pallas as pl
from jax.experimental.pallas import tpu as pltpu
from jax.sharding import PartitionSpec as P

BANDS = 16


highest = lax.Precision.HIGHEST
two_pi = 2.0 * math.pi


def from_behind(value, axis, steps):
    count = lax.axis_size(axis)
    leading, last = (max(0, -steps), min(count, count - steps))
    return lax.ppermute(value, axis, [(source, source + steps) for source in range(leading, last)])


def features(positions, length):
    frequency = 2 ** jnp.arange(BANDS, dtype=jnp.int32) + 1
    phases = positions[:, None] * frequency[None, :] % length
    angles = phases.astype(jnp.float32) * (two_pi / length)
    ramp_col = positions.astype(jnp.float32)[:, None] / length
    return jnp.concatenate([ramp_col, jnp.cos(angles), jnp.sin(angles)], axis=1)


def filter_forward(positions, length, weight_first, weight_second, weight_third, decay_rate):
    embedding = features(positions, length)
    pre_one = jnp.dot(
        embedding, weight_first, precision=highest, preferred_element_type=jnp.float32
    )
    act_one = jnp.sin(pre_one)
    pre_two = jnp.dot(act_one, weight_second, precision=highest, preferred_element_type=jnp.float32)
    act_two = jnp.sin(pre_two)
    shaped = jnp.dot(act_two, weight_third, precision=highest, preferred_element_type=jnp.float32)
    scaling = jnp.sqrt(jnp.expm1(-2.0 * decay_rate) / jnp.expm1(-2.0 * length * decay_rate))
    window = scaling[None, :] * jnp.exp(
        -decay_rate[None, :] * positions.astype(jnp.float32)[:, None]
    )
    return (shaped * window, (window, embedding, pre_one, act_one, pre_two, act_two))


def filter_head(grad_filter, saved_acts, weight_third):
    window, embedding, pre_one, act_one, pre_two, act_two = saved_acts
    grad_shaped = grad_filter * window
    grad_third = jnp.dot(
        act_two.T, grad_shaped, precision=highest, preferred_element_type=jnp.float32
    )
    grad_act_two = jnp.dot(
        grad_shaped, weight_third.T, precision=highest, preferred_element_type=jnp.float32
    )
    return (grad_third, grad_act_two)


def filter_tail(grad_act_two, saved_acts, weight_second):
    window, embedding, pre_one, act_one, pre_two, act_two = saved_acts
    grad_pre_two = grad_act_two * jnp.cos(pre_two)
    grad_second = jnp.dot(
        act_one.T, grad_pre_two, precision=highest, preferred_element_type=jnp.float32
    )
    grad_act_one = jnp.dot(
        grad_pre_two, weight_second.T, precision=highest, preferred_element_type=jnp.float32
    )
    grad_pre_one = grad_act_one * jnp.cos(pre_one)
    grad_first = jnp.dot(
        embedding.T, grad_pre_one, precision=highest, preferred_element_type=jnp.float32
    )
    return (grad_first, grad_second)


def rotation(first_index, second_index, modulus):
    phases = first_index * second_index % modulus
    angles = phases.astype(jnp.float32) * (two_pi / modulus)
    return (jnp.cos(angles), jnp.sin(angles))


def lane_forward(lane_rows, seq_count, points):
    width, length = lane_rows.shape
    depth_rows = length // seq_count
    blocks = lane_rows.reshape(width, seq_count, depth_rows)
    source_index = jnp.arange(seq_count, dtype=jnp.int32)
    lane_index = jnp.arange(2 * seq_count, dtype=jnp.int32)
    cosine_part, sine_part = rotation(lane_index[:, None], source_index[None, :], 2 * seq_count)
    small_table = jnp.concatenate([cosine_part, -sine_part], axis=0)
    product = jnp.einsum("kn,cnm->ckm", small_table, blocks, precision=highest)
    real_part = product[:, : 2 * seq_count]
    imag_part = product[:, 2 * seq_count :]
    cos_twist, sin_twist = rotation(
        lane_index[:, None], jnp.arange(depth_rows, dtype=jnp.int32)[None, :], points
    )
    turned = jnp.stack(
        [
            real_part * cos_twist + imag_part * sin_twist,
            imag_part * cos_twist - real_part * sin_twist,
        ]
    )
    grid_index = jnp.arange(depth_rows, dtype=jnp.int32)
    cos_block, sin_block = rotation(grid_index[:, None], grid_index[None, :], depth_rows)
    tables = jnp.concatenate([cos_block, sin_block], axis=1)
    both_parts = jnp.einsum("rckm,mj->rckj", turned, tables, precision=highest)
    return jnp.stack(
        [
            both_parts[0, :, :, :depth_rows] + both_parts[1, :, :, depth_rows:],
            both_parts[1, :, :, :depth_rows] - both_parts[0, :, :, depth_rows:],
        ]
    )


def lane_inverse(spectrum, seq_count, points):
    width = spectrum.shape[1]
    depth_rows = spectrum.shape[3]
    grid_index = jnp.arange(depth_rows, dtype=jnp.int32)
    cos_block, sin_block = rotation(grid_index[:, None], grid_index[None, :], depth_rows)
    tables = jnp.concatenate([cos_block, sin_block], axis=1)
    both_parts = jnp.einsum("rckm,mj->rckj", spectrum, tables, precision=highest)
    real_part = both_parts[0, :, :, :depth_rows] - both_parts[1, :, :, depth_rows:]
    imag_part = both_parts[1, :, :, :depth_rows] + both_parts[0, :, :, depth_rows:]
    lane_index = jnp.arange(2 * seq_count, dtype=jnp.int32)
    cos_twist, sin_twist = rotation(lane_index[:, None], grid_index[None, :], points)
    turned = jnp.stack(
        [
            real_part * cos_twist - imag_part * sin_twist,
            imag_part * cos_twist + real_part * sin_twist,
        ]
    )
    source_index = jnp.arange(seq_count, dtype=jnp.int32)
    cosine_part, sine_part = rotation(source_index[:, None], lane_index[None, :], 2 * seq_count)
    back_table = jnp.stack([cosine_part, -sine_part]) / points
    result_rows = jnp.einsum("rnk,rckm->cnm", back_table, turned, precision=highest)
    return result_rows.reshape(width, seq_count * depth_rows)


def pointwise(spectra):
    keyed_spec, filter_spec, grad_spec = spectra
    conv_spec = jnp.stack(
        [
            keyed_spec[0] * filter_spec[0] - keyed_spec[1] * filter_spec[1],
            keyed_spec[0] * filter_spec[1] + keyed_spec[1] * filter_spec[0],
        ]
    )
    back_spec = jnp.stack(
        [
            filter_spec[0] * grad_spec[0] + filter_spec[1] * grad_spec[1],
            filter_spec[0] * grad_spec[1] - filter_spec[1] * grad_spec[0],
        ]
    )
    shape_spec = jnp.stack(
        [
            keyed_spec[0] * grad_spec[0] + keyed_spec[1] * grad_spec[1],
            keyed_spec[0] * grad_spec[1] - keyed_spec[1] * grad_spec[0],
        ]
    )
    return (conv_spec, back_spec, shape_spec)


def per_device(
    tokens,
    embed_table,
    short_conv,
    query_branch,
    key_branch,
    decay_rate,
    weight_first,
    weight_second,
    weight_third,
    skip_gain,
    cotangent,
):
    seq_count = lax.axis_size("seq")
    seq_index = lax.axis_index("seq")
    row_count = query_branch.shape[0]
    chan_width = query_branch.shape[1]
    length = row_count * seq_count
    points = 2 * length
    inv_root = 1.0 / math.sqrt(length)
    vocab_size = embed_table.shape[0]
    earlier = from_behind(tokens[row_count - 2 :], "seq", 1)
    window_ids = jnp.concatenate([earlier, tokens])
    row_start = seq_index * row_count
    window_pos = row_start + jnp.arange(row_count + 2, dtype=jnp.int32) - 2
    present = window_pos >= 0
    vocab_ids = jnp.arange(vocab_size, dtype=jnp.int32)
    lookup = ((window_ids[:, None] == vocab_ids[None, :]) & present[:, None]).astype(jnp.bfloat16)
    embedded = jnp.dot(lookup, embed_table, preferred_element_type=jnp.float32)
    value_branch = (
        short_conv[0] * embedded[2:]
        + short_conv[1] * embedded[1:-1]
        + short_conv[2] * embedded[:-2]
    )
    key_rows = key_branch.astype(jnp.float32)
    keyed_value = key_rows * value_branch
    query_rows = query_branch.astype(jnp.float32)
    grad_out = cotangent.astype(jnp.float32)
    grad_z = grad_out * query_rows
    slice_width = chan_width // seq_count
    chan_start = seq_index * slice_width
    third_slice = lax.dynamic_slice_in_dim(weight_third, chan_start, slice_width, 1)
    rate_slice = lax.dynamic_slice_in_dim(decay_rate, chan_start, slice_width, 0)
    all_positions = jnp.arange(length, dtype=jnp.int32)
    filter_full, tail_acts = filter_forward(
        all_positions, length, weight_first, weight_second, third_slice, rate_slice
    )
    keyed_lanes, grad_lanes = (
        lax.all_to_all(keyed_value.T, "seq", split_axis=0, concat_axis=1, tiled=True),
        lax.all_to_all(grad_z.T, "seq", split_axis=0, concat_axis=1, tiled=True),
    )
    spectra = (
        lane_forward(keyed_lanes, seq_count, points),
        lane_forward(filter_full.T, seq_count, points),
        lane_forward(grad_lanes, seq_count, points),
    )
    conv_spec, back_spec, shape_spec = pointwise(spectra)
    conv_lanes = lane_inverse(conv_spec, seq_count, points)
    back_lanes = lane_inverse(back_spec, seq_count, points)
    filter_lanes = lane_inverse(shape_spec, seq_count, points)
    conv_rows, back_rows = (
        lax.all_to_all(conv_lanes, "seq", split_axis=1, concat_axis=0, tiled=True),
        lax.all_to_all(back_lanes, "seq", split_axis=1, concat_axis=0, tiled=True),
    )
    convolved = conv_rows.T
    back_keyed = back_rows.T
    third_small, act_two_part = filter_head(filter_lanes.T, tail_acts, third_slice)
    third_part = lax.dynamic_update_slice(
        jnp.zeros((third_small.shape[0], chan_width), jnp.float32),
        third_small,
        (jnp.zeros((), jnp.int32), chan_start),
    )
    inner_sum = convolved + skip_gain * keyed_value
    operator_out = (query_rows * inner_sum).astype(jnp.bfloat16)
    grad_query = (grad_out * inner_sum).astype(jnp.bfloat16)
    grad_keyed = back_keyed + skip_gain * grad_z
    grad_key = (grad_keyed * value_branch).astype(jnp.bfloat16)
    grad_value = grad_keyed * key_rows
    short_part = jnp.stack(
        [
            jnp.sum(grad_value * embedded[2 - offset : 2 - offset + row_count], axis=0)
            for offset in range(3)
        ]
    )
    skip_part = jnp.sum(grad_z * keyed_value, axis=0)
    ids_stacked = jnp.concatenate([window_ids[2:], window_ids[1:-1], window_ids[:-2]])
    live_stacked = jnp.concatenate([present[2:], present[1:-1], present[:-2]])
    weighted = jnp.concatenate([short_conv[offset] * grad_value for offset in range(3)], axis=0)
    vocab_rows = jnp.arange(vocab_size // seq_count * lax.axis_size("seq"), dtype=jnp.int32)
    matches = ((vocab_rows[:, None] == ids_stacked[None, :]) & live_stacked[None, :]).astype(
        jnp.float32
    )
    grad_embed = (
        lax.psum_scatter(
            jnp.dot(matches, weighted, precision=highest, preferred_element_type=jnp.float32),
            "seq",
            scatter_dimension=0,
            tiled=True,
        )
        * inv_root
    )
    grad_act_two = lax.psum(act_two_part, "chan")
    first_part, second_part = filter_tail(grad_act_two, tail_acts, weight_second)
    grad_short, grad_skip, grad_third, grad_first, grad_second = lax.psum(
        (short_part, skip_part, third_part, first_part, second_part), "seq"
    )
    return (
        operator_out,
        grad_query,
        grad_key,
        grad_embed,
        grad_short * inv_root,
        grad_skip * inv_root,
        grad_first * inv_root,
        grad_second * inv_root,
        grad_third * inv_root,
    )

MESH = pl.DeviceIdType.MESH
f32 = jnp.float32
bf16 = jnp.bfloat16


def table_split(table):
    high = table.astype(ml_dtypes.bfloat16)
    return high, (table - high.astype(np.float32)).astype(ml_dtypes.bfloat16)


def split(value):
    high = value.astype(bf16)
    return high, (value - high.astype(f32)).astype(bf16)


def dot(left, right):
    return jnp.dot(left, right, preferred_element_type=f32)


def dot_full(left, right, contract=((1,), (0,))):
    return lax.dot_general(
        left, right, (contract, ((), ())), precision=highest, preferred_element_type=f32
    )


def low_lanes(shape):
    return lax.broadcasted_iota(jnp.int32, shape, len(shape) - 1) < shape[-1] // 2


def swap(value):
    return pltpu.roll(value, value.shape[-1] // 2, value.ndim - 1)


def greet(devices):
    barrier = pltpu.get_barrier_semaphore()
    for device in devices:
        pl.semaphore_signal(barrier, inc=1, device_id=device, device_id_type=MESH)
    pl.semaphore_wait(barrier, len(devices))


def pack_rows(number, query, key, cotangent, out, base):
    lanes = out.shape[-1]
    block = number // 2 * lanes
    key_part = key[:, block : block + lanes].astype(f32)
    grad_part = cotangent[:, block : block + lanes].astype(f32) * query[
        :, block : block + lanes
    ].astype(f32)
    low = low_lanes(key_part.shape)
    if number % 2 == 0:
        packed = jnp.where(low, key_part, swap(grad_part))
    else:
        packed = jnp.where(low, swap(key_part), grad_part)
    out[number, : key.shape[0]] = packed


def send_kernel(count, tokens, query, key, cotangent, out, staged, send_sem, recv_sem, own_sem):
    me = lax.axis_index("seq")
    chan = lax.axis_index("chan")
    rows = key.shape[0]
    token_rows = tokens[...].astype(f32)
    for number in range(count):
        pack_rows(number, query, key, cotangent, staged, 0)
        staged[number, rows:] = jnp.zeros((staged.shape[1] - rows, staged.shape[2]), f32)
        staged[number, rows : rows + token_rows.shape[0]] = token_rows
    greet([(lax.rem(me + step, count), chan) for step in range(1, count)])
    copies = []
    for step in range(1, count):
        peer = lax.rem(me + step, count)
        copies.append(
            pltpu.make_async_remote_copy(
                src_ref=staged.at[peer],
                dst_ref=out.at[me],
                send_sem=send_sem.at[step],
                recv_sem=recv_sem.at[step],
                device_id=(peer, chan),
                device_id_type=MESH,
            )
        )
    for copy in copies:
        copy.start()
    own = pltpu.make_async_copy(staged.at[me], out.at[me], own_sem)
    own.start()
    own.wait()
    for copy in copies:
        copy.wait()


def conv_kernel(
    count,
    rows,
    coefs,
    arrived,
    params,
    first,
    second,
    feats,
    twiddles,
    table_high,
    table_low,
    pay,
    hidden,
    state,
    filters,
    total,
    shape_total,
    value,
    embedded,
    gated,
    onehot,
    acts,
    windows,
):
    lanes = params.shape[1]
    half = lanes // 2
    vocab = onehot.shape[0]
    length = count * rows
    low = low_lanes((rows, lanes))
    sign = jnp.where(low, 1.0, -1.0).astype(f32)
    third = params[vocab : vocab + 64]
    top = vocab + 64
    rate, scale, skip = params[top : top + 1], params[top + 1 : top + 2], params[top + 2 : top + 3]
    taps = [params[top + 3 + j : top + 4 + j] for j in range(3)]
    table = params[:vocab].astype(bf16)

    pre_one = dot_full(first[...], feats[...], ((0,), (0,)))
    act_one = jnp.sin(pre_one)
    acts[0] = act_one
    acts[1] = jnp.cos(pre_one)
    pre_two = dot_full(second[...], act_one, ((0,), (0,)))
    acts[2] = jnp.sin(pre_two)
    acts[3] = jnp.cos(pre_two)

    embedded[:8] = jnp.zeros((8, lanes), f32)
    row_ids = lax.broadcasted_iota(jnp.int32, (rows, lanes), 0).astype(f32)
    vocab_ids = lax.broadcasted_iota(jnp.int32, (vocab, lanes), 0).astype(f32)
    for block in range(count):
        act_rows = acts[2, :, block * rows : (block + 1) * rows].T
        window = scale * jnp.exp(-rate * (row_ids + float(block * rows)))
        windows[block] = window
        filters[block] = dot_full(act_rows, third) * window
        for piece in range(rows // lanes):
            ids = arrived[block, rows + piece : rows + piece + 1]
            matches = jnp.where(vocab_ids == ids, 1.0, 0.0)
            start = block * rows + piece * lanes
            onehot[:, start : start + lanes] = matches.astype(bf16)
            embedded[8 + start : 8 + start + lanes] = dot(matches.T.astype(bf16), table)
    for block in range(count):
        start = 8 + block * rows
        branch = (
            taps[0] * embedded[start : start + rows]
            + taps[1] * embedded[start - 1 : start - 1 + rows]
            + taps[2] * embedded[start - 2 : start - 2 + rows]
        )
        value[block] = branch
        packed = arrived[block, :rows]
        state[block] = jnp.where(low, packed * branch, packed)
    total[...] = jnp.zeros_like(total)
    shape_total[...] = jnp.zeros_like(shape_total)

    def spread(both):
        high, rest = split(both)
        product = (
            dot(table_high[...], high) + dot(table_high[...], rest) + dot(table_low[...], high)
        )
        return product[:rows], product[rows:]

    def one(lane, carry):
        cos_t = twiddles[lane, 0]
        sin_t = twiddles[lane, 1]

        def forward(ref):
            real = jnp.zeros((rows, lanes), f32)
            imag = jnp.zeros((rows, lanes), f32)
            for n in range(count):
                piece = ref[n]
                real = real + coefs[lane, n] * piece
                imag = imag - coefs[lane, count + n] * piece
            turned = jnp.concatenate(
                [real * cos_t + imag * sin_t, imag * cos_t - real * sin_t], axis=1
            )
            by_cos, by_sin = spread(turned)
            return (
                by_cos[:, :lanes] + by_sin[:, lanes:],
                by_cos[:, lanes:] - by_sin[:, :lanes],
            )

        xr, xi = forward(state)
        fr, fi = forward(filters)
        fi = fi * sign
        by_cos, by_sin = spread(jnp.concatenate([xr * fr - xi * fi, xr * fi + xi * fr], axis=1))
        zr = by_cos[:, :lanes] - by_sin[:, lanes:]
        zi = by_cos[:, lanes:] + by_sin[:, :lanes]
        ur = zr * cos_t - zi * sin_t
        ui = zr * sin_t + zi * cos_t
        gr, gi = swap(xr), swap(xi)
        hr = xr * gr + xi * gi
        hi = xr * gi - xi * gr
        by_cos, by_sin = spread(jnp.where(low, hr, swap(hi)))
        both = by_cos - sign * swap(by_sin)
        part_cos = both * jnp.where(low, cos_t, -sin_t)
        part_sin = both * jnp.where(low, sin_t, cos_t)
        for n in range(count):
            cosine = coefs[lane, 2 * count + n]
            sine = coefs[lane, 3 * count + n]
            total[n] += cosine * ur - sine * ui
            shape_total[n] += cosine * part_cos - sine * part_sin
        return carry

    lax.fori_loop(0, count + 1, one, 0)

    gated[length:] = jnp.zeros((8, lanes), f32)
    short_sums = [jnp.zeros((1, lanes), f32) for _ in range(3)]
    skip_sum = jnp.zeros((1, lanes), f32)
    third_sum = jnp.zeros((64, lanes), f32)
    for block in range(count):
        mine = state[block]
        summed = total[block] + skip * mine
        pay[block, :rows] = jnp.where(low, summed, summed * value[block])
        grad_value = summed * swap(arrived[block, :rows])
        start = block * rows
        gated[start : start + rows] = grad_value
        for j in range(3):
            short_sums[j] += jnp.sum(
                grad_value * embedded[8 + start - j : 8 + start - j + rows], axis=0, keepdims=True
            )
        skip_sum += jnp.sum(mine * swap(mine), axis=0, keepdims=True)
        grad_rows = shape_total[block]
        grad_rows = (grad_rows + swap(grad_rows)) * windows[block]
        columns = pl.ds(start, rows)
        third_sum += dot_full(acts[2, :, columns], grad_rows)
        grad_act = dot_full(jnp.where(low_lanes(third.shape), third, 0.0), grad_rows, ((1,), (1,)))
        acts[3, :, columns] = grad_act * acts[3, :, columns]
    embed_sum = jnp.zeros((vocab, lanes), f32)
    for block in range(count):
        start = block * rows
        spread_rows = (
            taps[0] * gated[start : start + rows]
            + taps[1] * gated[start + 1 : start + 1 + rows]
            + taps[2] * gated[start + 2 : start + 2 + rows]
        )
        high, rest = split(spread_rows)
        matches = onehot[:, start : start + rows]
        embed_sum += dot(matches, high) + dot(matches, rest)
    inv_root = 1.0 / math.sqrt(length)
    grad_pre_two = acts[3]
    grad_second = dot_full(acts[0], grad_pre_two, ((1,), (1,))) * inv_root
    grad_pre_one = dot_full(second[...], grad_pre_two) * acts[1]
    grad_first = dot_full(feats[...], grad_pre_one, ((1,), (1,))) * inv_root
    hidden[:64] = grad_second
    hidden[64:] = grad_first
    share = vocab // count
    small = jnp.concatenate(
        [third_sum, *short_sums, skip_sum, jnp.zeros((4, lanes), f32)], axis=0
    ) * inv_root
    for block in range(count):
        pay[block, rows : rows + share] = embed_sum[block * share : (block + 1) * share] * inv_root
        pay[block, rows + share :] = small


def return_kernel(
    count,
    groups,
    pay,
    hidden,
    query,
    cotangent,
    out,
    grad_query,
    grad_key,
    grad_embed,
    small,
    summed,
    landed,
    by_chan,
    by_seq,
    held,
    send_sem,
    recv_sem,
    own_sem,
    chan_send,
    chan_recv,
    seq_send,
    seq_recv,
):
    me = lax.axis_index("seq")
    chan = lax.axis_index("chan")
    rows = query.shape[0]
    lanes = pay.shape[2]
    share = grad_embed.shape[0]
    peers = [(lax.rem(me + step, count), chan) for step in range(1, count)]
    across = [(me, lax.rem(chan + step, groups)) for step in range(1, groups)]
    greet(peers + across)

    def post(source, target, send, recv, device):
        copy = pltpu.make_async_remote_copy(
            src_ref=source,
            dst_ref=target,
            send_sem=send,
            recv_sem=recv,
            device_id=device,
            device_id_type=MESH,
        )
        copy.start()
        return copy

    wide = [
        post(hidden, by_chan.at[n], chan_send.at[n], chan_recv.at[n], device)
        for n, device in enumerate(across)
    ]
    main = [
        post(pay.at[device[0]], landed.at[me], send_sem.at[n], recv_sem.at[n], device)
        for n, device in enumerate(peers)
    ]
    own = pltpu.make_async_copy(pay.at[me], landed.at[me], own_sem)
    own.start()
    for copy in wide:
        copy.wait()
    group_sum = hidden[...]
    for n in range(groups - 1):
        group_sum = group_sum + by_chan[n]
    held[...] = group_sum
    along = [
        post(held, by_seq.at[me], seq_send.at[n], seq_recv.at[n], device)
        for n, device in enumerate(peers)
    ]
    by_seq[me] = group_sum
    own.wait()
    for copy in main:
        copy.wait()
    for block in range(count // 2):
        columns = pl.ds(block * lanes, lanes)
        even, odd = landed[2 * block], landed[2 * block + 1]
        low = low_lanes((rows, lanes))
        inner = jnp.where(low, even[:rows], swap(odd[:rows]))
        out[:, columns] = (query[:, columns].astype(f32) * inner).astype(bf16)
        grad_query[:, columns] = (cotangent[:, columns].astype(f32) * inner).astype(bf16)
        grad_key[:, columns] = jnp.where(low, swap(even[:rows]), odd[:rows]).astype(bf16)
        rest_even, rest_odd = even[rows:], odd[rows:]
        rest = jnp.where(low_lanes(rest_even.shape), swap(rest_even), rest_odd)
        grad_embed[:, columns] = rest[:share]
        small[:, columns] = rest[share:]
    for copy in along:
        copy.wait()
    everything = by_seq[0]
    for n in range(1, count):
        everything = everything + by_seq[n]
    summed[...] = everything


def feature_table(length):
    positions = np.arange(length, dtype=np.int64)
    frequency = 2 ** np.arange(BANDS, dtype=np.int64) + 1
    phases = positions[:, None] * frequency[None, :] % length
    angles = phases.astype(np.float32) * np.float32(two_pi / length)
    ramp = positions.astype(np.float32)[:, None] / np.float32(length)
    return np.concatenate([ramp, np.cos(angles), np.sin(angles)], axis=1).T.astype(np.float32)


def fused_device(
    tokens,
    embed_table,
    short_conv,
    query_branch,
    key_branch,
    decay_rate,
    weight_first,
    weight_second,
    weight_third,
    skip_gain,
    cotangent,
):
    count = lax.axis_size("seq")
    groups = lax.axis_size("chan")
    seq_index = lax.axis_index("seq")
    rows, chan_width = query_branch.shape
    length = rows * count
    points = 2 * length
    vocab = embed_table.shape[0]
    hidden_units = weight_second.shape[0]
    feat = weight_first.shape[0]
    slice_width = chan_width // count
    lanes = 2 * slice_width
    share = vocab // count
    scaling = jnp.sqrt(jnp.expm1(-2.0 * decay_rate) / jnp.expm1(-2.0 * length * decay_rate))
    stacked = jnp.concatenate(
        [
            embed_table.astype(f32),
            weight_third,
            decay_rate[None],
            scaling[None],
            skip_gain[None],
            short_conv,
            jnp.zeros((2, chan_width), f32),
        ],
        axis=0,
    )
    mine = lax.dynamic_slice_in_dim(stacked, seq_index * slice_width, slice_width, 1)
    params = jnp.concatenate([mine, mine], axis=1)

    vmem = pl.BlockSpec(memory_space=pltpu.VMEM)
    smem = pl.BlockSpec(memory_space=pltpu.SMEM)
    dma = pltpu.SemaphoreType.DMA
    arrived_rows = rows + 8
    arrived = pl.pallas_call(
        functools.partial(send_kernel, count),
        out_shape=jax.ShapeDtypeStruct((count, arrived_rows, lanes), f32),
        in_specs=[vmem] * 4,
        out_specs=vmem,
        scratch_shapes=[
            pltpu.VMEM((count, arrived_rows, lanes), f32),
            dma((count,)),
            dma((count,)),
            dma(()),
        ],
        compiler_params=pltpu.CompilerParams(
            collective_id=0, has_side_effects=True, vmem_limit_bytes=32 * 2**20
        ),
        name="send_slices",
    )(tokens.reshape(rows // lanes, lanes), query_branch, key_branch, cotangent)

    depth = np.arange(rows)
    turns = np.arange(count + 1)
    angle = two_pi * (depth[:, None] * depth[None, :] % rows) / rows
    tables = np.concatenate([np.cos(angle), np.sin(angle)], axis=0).astype(np.float32)
    table_high, table_low = table_split(tables)
    twist = two_pi * (turns[:, None] * depth[None, :]) / points
    twiddles = np.stack([np.cos(twist), np.sin(twist)], axis=1).astype(np.float32)
    twiddles = jnp.broadcast_to(jnp.asarray(twiddles)[..., None], (count + 1, 2, rows, lanes))
    small_angle = two_pi * (turns[:, None] * np.arange(count)[None, :] % (2 * count)) / (2 * count)
    weight = np.where((turns == 0) | (turns == count), 1.0, 2.0)[:, None] / points
    coefs = np.concatenate(
        [
            np.cos(small_angle),
            np.sin(small_angle),
            weight * np.cos(small_angle),
            weight * np.sin(small_angle),
        ],
        axis=1,
    ).astype(np.float32)
    pay_rows = rows + share + hidden_units + 8
    pay, hidden = pl.pallas_call(
        functools.partial(conv_kernel, count, rows),
        out_shape=(
            jax.ShapeDtypeStruct((count, pay_rows, lanes), f32),
            jax.ShapeDtypeStruct((hidden_units + feat, hidden_units), f32),
        ),
        in_specs=[smem] + [vmem] * 8,
        out_specs=(vmem, vmem),
        scratch_shapes=[
            pltpu.VMEM((count, rows, lanes), f32),
            pltpu.VMEM((count, rows, lanes), f32),
            pltpu.VMEM((count, rows, lanes), f32),
            pltpu.VMEM((count, rows, lanes), f32),
            pltpu.VMEM((count, rows, lanes), f32),
            pltpu.VMEM((length + 8, lanes), f32),
            pltpu.VMEM((length + 8, lanes), f32),
            pltpu.VMEM((vocab, length), bf16),
            pltpu.VMEM((4, hidden_units, length), f32),
            pltpu.VMEM((count, rows, lanes), f32),
        ],
        compiler_params=pltpu.CompilerParams(vmem_limit_bytes=48 * 2**20),
        name="convolve_slices",
    )(
        jnp.asarray(coefs),
        arrived,
        params,
        weight_first,
        weight_second,
        jnp.asarray(feature_table(length)),
        twiddles,
        jnp.asarray(table_high),
        jnp.asarray(table_low),
    )
    hidden_shape = (hidden_units + feat, hidden_units)
    out, grad_query, grad_key, grad_embed, small, summed = pl.pallas_call(
        functools.partial(return_kernel, count, groups),
        out_shape=(
            jax.ShapeDtypeStruct((rows, chan_width), bf16),
            jax.ShapeDtypeStruct((rows, chan_width), bf16),
            jax.ShapeDtypeStruct((rows, chan_width), bf16),
            jax.ShapeDtypeStruct((share, chan_width), f32),
            jax.ShapeDtypeStruct((hidden_units + 8, chan_width), f32),
            jax.ShapeDtypeStruct(hidden_shape, f32),
        ),
        in_specs=[vmem] * 4,
        out_specs=(vmem,) * 6,
        scratch_shapes=[
            pltpu.VMEM((count, pay_rows, lanes), f32),
            pltpu.VMEM((groups,) + hidden_shape, f32),
            pltpu.VMEM((count,) + hidden_shape, f32),
            pltpu.VMEM(hidden_shape, f32),
            dma((count,)),
            dma((count,)),
            dma(()),
            dma((groups,)),
            dma((groups,)),
            dma((count,)),
            dma((count,)),
        ],
        compiler_params=pltpu.CompilerParams(
            collective_id=1, has_side_effects=True, vmem_limit_bytes=32 * 2**20
        ),
        name="return_slices",
    )(pay, hidden, query_branch, cotangent)
    return (
        out,
        grad_query,
        grad_key,
        grad_embed,
        small[hidden_units : hidden_units + 3],
        small[hidden_units + 3],
        summed[hidden_units:],
        summed[:hidden_units],
        small[:hidden_units],
    )


def per_slice(*arrays):
    packed_width = 2 * arrays[3].shape[1] // lax.axis_size("seq")
    body = fused_device if packed_width % 128 == 0 else per_device
    return body(*arrays)


def solution(mesh):
    in_specs = (
        P("seq"),
        P(None, "chan"),
        P(None, "chan"),
        P("seq", "chan"),
        P("seq", "chan"),
        P("chan"),
        P(),
        P(),
        P(None, "chan"),
        P("chan"),
        P("seq", "chan"),
    )
    out_specs = (
        P("seq", "chan"),
        P("seq", "chan"),
        P("seq", "chan"),
        P("seq", "chan"),
        P(None, "chan"),
        P("chan"),
        P(),
        P(),
        P(None, "chan"),
    )
    return jax.shard_map(
        per_slice, mesh=mesh, in_specs=in_specs, out_specs=out_specs, check_vma=False
    )
```

```python
import functools
import math

import jax
import jax.numpy as jnp
import ml_dtypes
import numpy as np
from jax import lax
from jax.experimental import pallas as pl
from jax.experimental.pallas import tpu as pltpu
from jax.sharding import PartitionSpec as P

BANDS = 16


highest = lax.Precision.HIGHEST
two_pi = 2.0 * math.pi


def from_behind(value, axis, steps):
    count = lax.axis_size(axis)
    leading, last = (max(0, -steps), min(count, count - steps))
    return lax.ppermute(value, axis, [(source, source + steps) for source in range(leading, last)])


def features(positions, length):
    frequency = 2 ** jnp.arange(BANDS, dtype=jnp.int32) + 1
    phases = positions[:, None] * frequency[None, :] % length
    angles = phases.astype(jnp.float32) * (two_pi / length)
    ramp_col = positions.astype(jnp.float32)[:, None] / length
    return jnp.concatenate([ramp_col, jnp.cos(angles), jnp.sin(angles)], axis=1)


def filter_forward(positions, length, weight_first, weight_second, weight_third, decay_rate):
    embedding = features(positions, length)
    pre_one = jnp.dot(
        embedding, weight_first, precision=highest, preferred_element_type=jnp.float32
    )
    act_one = jnp.sin(pre_one)
    pre_two = jnp.dot(act_one, weight_second, precision=highest, preferred_element_type=jnp.float32)
    act_two = jnp.sin(pre_two)
    shaped = jnp.dot(act_two, weight_third, precision=highest, preferred_element_type=jnp.float32)
    scaling = jnp.sqrt(jnp.expm1(-2.0 * decay_rate) / jnp.expm1(-2.0 * length * decay_rate))
    window = scaling[None, :] * jnp.exp(
        -decay_rate[None, :] * positions.astype(jnp.float32)[:, None]
    )
    return (shaped * window, (window, embedding, pre_one, act_one, pre_two, act_two))


def filter_head(grad_filter, saved_acts, weight_third):
    window, embedding, pre_one, act_one, pre_two, act_two = saved_acts
    grad_shaped = grad_filter * window
    grad_third = jnp.dot(
        act_two.T, grad_shaped, precision=highest, preferred_element_type=jnp.float32
    )
    grad_act_two = jnp.dot(
        grad_shaped, weight_third.T, precision=highest, preferred_element_type=jnp.float32
    )
    return (grad_third, grad_act_two)


def filter_tail(grad_act_two, saved_acts, weight_second):
    window, embedding, pre_one, act_one, pre_two, act_two = saved_acts
    grad_pre_two = grad_act_two * jnp.cos(pre_two)
    grad_second = jnp.dot(
        act_one.T, grad_pre_two, precision=highest, preferred_element_type=jnp.float32
    )
    grad_act_one = jnp.dot(
        grad_pre_two, weight_second.T, precision=highest, preferred_element_type=jnp.float32
    )
    grad_pre_one = grad_act_one * jnp.cos(pre_one)
    grad_first = jnp.dot(
        embedding.T, grad_pre_one, precision=highest, preferred_element_type=jnp.float32
    )
    return (grad_first, grad_second)


def rotation(first_index, second_index, modulus):
    phases = first_index * second_index % modulus
    angles = phases.astype(jnp.float32) * (two_pi / modulus)
    return (jnp.cos(angles), jnp.sin(angles))


def lane_forward(lane_rows, seq_count, points):
    width, length = lane_rows.shape
    depth_rows = length // seq_count
    blocks = lane_rows.reshape(width, seq_count, depth_rows)
    source_index = jnp.arange(seq_count, dtype=jnp.int32)
    lane_index = jnp.arange(2 * seq_count, dtype=jnp.int32)
    cosine_part, sine_part = rotation(lane_index[:, None], source_index[None, :], 2 * seq_count)
    small_table = jnp.concatenate([cosine_part, -sine_part], axis=0)
    product = jnp.einsum("kn,cnm->ckm", small_table, blocks, precision=highest)
    real_part = product[:, : 2 * seq_count]
    imag_part = product[:, 2 * seq_count :]
    cos_twist, sin_twist = rotation(
        lane_index[:, None], jnp.arange(depth_rows, dtype=jnp.int32)[None, :], points
    )
    turned = jnp.stack(
        [
            real_part * cos_twist + imag_part * sin_twist,
            imag_part * cos_twist - real_part * sin_twist,
        ]
    )
    grid_index = jnp.arange(depth_rows, dtype=jnp.int32)
    cos_block, sin_block = rotation(grid_index[:, None], grid_index[None, :], depth_rows)
    tables = jnp.concatenate([cos_block, sin_block], axis=1)
    both_parts = jnp.einsum("rckm,mj->rckj", turned, tables, precision=highest)
    return jnp.stack(
        [
            both_parts[0, :, :, :depth_rows] + both_parts[1, :, :, depth_rows:],
            both_parts[1, :, :, :depth_rows] - both_parts[0, :, :, depth_rows:],
        ]
    )


def lane_inverse(spectrum, seq_count, points):
    width = spectrum.shape[1]
    depth_rows = spectrum.shape[3]
    grid_index = jnp.arange(depth_rows, dtype=jnp.int32)
    cos_block, sin_block = rotation(grid_index[:, None], grid_index[None, :], depth_rows)
    tables = jnp.concatenate([cos_block, sin_block], axis=1)
    both_parts = jnp.einsum("rckm,mj->rckj", spectrum, tables, precision=highest)
    real_part = both_parts[0, :, :, :depth_rows] - both_parts[1, :, :, depth_rows:]
    imag_part = both_parts[1, :, :, :depth_rows] + both_parts[0, :, :, depth_rows:]
    lane_index = jnp.arange(2 * seq_count, dtype=jnp.int32)
    cos_twist, sin_twist = rotation(lane_index[:, None], grid_index[None, :], points)
    turned = jnp.stack(
        [
            real_part * cos_twist - imag_part * sin_twist,
            imag_part * cos_twist + real_part * sin_twist,
        ]
    )
    source_index = jnp.arange(seq_count, dtype=jnp.int32)
    cosine_part, sine_part = rotation(source_index[:, None], lane_index[None, :], 2 * seq_count)
    back_table = jnp.stack([cosine_part, -sine_part]) / points
    result_rows = jnp.einsum("rnk,rckm->cnm", back_table, turned, precision=highest)
    return result_rows.reshape(width, seq_count * depth_rows)


def pointwise(spectra):
    keyed_spec, filter_spec, grad_spec = spectra
    conv_spec = jnp.stack(
        [
            keyed_spec[0] * filter_spec[0] - keyed_spec[1] * filter_spec[1],
            keyed_spec[0] * filter_spec[1] + keyed_spec[1] * filter_spec[0],
        ]
    )
    back_spec = jnp.stack(
        [
            filter_spec[0] * grad_spec[0] + filter_spec[1] * grad_spec[1],
            filter_spec[0] * grad_spec[1] - filter_spec[1] * grad_spec[0],
        ]
    )
    shape_spec = jnp.stack(
        [
            keyed_spec[0] * grad_spec[0] + keyed_spec[1] * grad_spec[1],
            keyed_spec[0] * grad_spec[1] - keyed_spec[1] * grad_spec[0],
        ]
    )
    return (conv_spec, back_spec, shape_spec)


def per_device(
    tokens,
    embed_table,
    short_conv,
    query_branch,
    key_branch,
    decay_rate,
    weight_first,
    weight_second,
    weight_third,
    skip_gain,
    cotangent,
):
    seq_count = lax.axis_size("seq")
    seq_index = lax.axis_index("seq")
    row_count = query_branch.shape[0]
    chan_width = query_branch.shape[1]
    length = row_count * seq_count
    points = 2 * length
    inv_root = 1.0 / math.sqrt(length)
    vocab_size = embed_table.shape[0]
    earlier = from_behind(tokens[row_count - 2 :], "seq", 1)
    window_ids = jnp.concatenate([earlier, tokens])
    row_start = seq_index * row_count
    window_pos = row_start + jnp.arange(row_count + 2, dtype=jnp.int32) - 2
    present = window_pos >= 0
    vocab_ids = jnp.arange(vocab_size, dtype=jnp.int32)
    lookup = ((window_ids[:, None] == vocab_ids[None, :]) & present[:, None]).astype(jnp.bfloat16)
    embedded = jnp.dot(lookup, embed_table, preferred_element_type=jnp.float32)
    value_branch = (
        short_conv[0] * embedded[2:]
        + short_conv[1] * embedded[1:-1]
        + short_conv[2] * embedded[:-2]
    )
    key_rows = key_branch.astype(jnp.float32)
    keyed_value = key_rows * value_branch
    query_rows = query_branch.astype(jnp.float32)
    grad_out = cotangent.astype(jnp.float32)
    grad_z = grad_out * query_rows
    slice_width = chan_width // seq_count
    chan_start = seq_index * slice_width
    third_slice = lax.dynamic_slice_in_dim(weight_third, chan_start, slice_width, 1)
    rate_slice = lax.dynamic_slice_in_dim(decay_rate, chan_start, slice_width, 0)
    all_positions = jnp.arange(length, dtype=jnp.int32)
    filter_full, tail_acts = filter_forward(
        all_positions, length, weight_first, weight_second, third_slice, rate_slice
    )
    keyed_lanes, grad_lanes = (
        lax.all_to_all(keyed_value.T, "seq", split_axis=0, concat_axis=1, tiled=True),
        lax.all_to_all(grad_z.T, "seq", split_axis=0, concat_axis=1, tiled=True),
    )
    spectra = (
        lane_forward(keyed_lanes, seq_count, points),
        lane_forward(filter_full.T, seq_count, points),
        lane_forward(grad_lanes, seq_count, points),
    )
    conv_spec, back_spec, shape_spec = pointwise(spectra)
    conv_lanes = lane_inverse(conv_spec, seq_count, points)
    back_lanes = lane_inverse(back_spec, seq_count, points)
    filter_lanes = lane_inverse(shape_spec, seq_count, points)
    conv_rows, back_rows = (
        lax.all_to_all(conv_lanes, "seq", split_axis=1, concat_axis=0, tiled=True),
        lax.all_to_all(back_lanes, "seq", split_axis=1, concat_axis=0, tiled=True),
    )
    convolved = conv_rows.T
    back_keyed = back_rows.T
    third_small, act_two_part = filter_head(filter_lanes.T, tail_acts, third_slice)
    third_part = lax.dynamic_update_slice(
        jnp.zeros((third_small.shape[0], chan_width), jnp.float32),
        third_small,
        (jnp.zeros((), jnp.int32), chan_start),
    )
    inner_sum = convolved + skip_gain * keyed_value
    operator_out = (query_rows * inner_sum).astype(jnp.bfloat16)
    grad_query = (grad_out * inner_sum).astype(jnp.bfloat16)
    grad_keyed = back_keyed + skip_gain * grad_z
    grad_key = (grad_keyed * value_branch).astype(jnp.bfloat16)
    grad_value = grad_keyed * key_rows
    short_part = jnp.stack(
        [
            jnp.sum(grad_value * embedded[2 - offset : 2 - offset + row_count], axis=0)
            for offset in range(3)
        ]
    )
    skip_part = jnp.sum(grad_z * keyed_value, axis=0)
    ids_stacked = jnp.concatenate([window_ids[2:], window_ids[1:-1], window_ids[:-2]])
    live_stacked = jnp.concatenate([present[2:], present[1:-1], present[:-2]])
    weighted = jnp.concatenate([short_conv[offset] * grad_value for offset in range(3)], axis=0)
    vocab_rows = jnp.arange(vocab_size // seq_count * lax.axis_size("seq"), dtype=jnp.int32)
    matches = ((vocab_rows[:, None] == ids_stacked[None, :]) & live_stacked[None, :]).astype(
        jnp.float32
    )
    grad_embed = (
        lax.psum_scatter(
            jnp.dot(matches, weighted, precision=highest, preferred_element_type=jnp.float32),
            "seq",
            scatter_dimension=0,
            tiled=True,
        )
        * inv_root
    )
    grad_act_two = lax.psum(act_two_part, "chan")
    first_part, second_part = filter_tail(grad_act_two, tail_acts, weight_second)
    grad_short, grad_skip, grad_third, grad_first, grad_second = lax.psum(
        (short_part, skip_part, third_part, first_part, second_part), "seq"
    )
    return (
        operator_out,
        grad_query,
        grad_key,
        grad_embed,
        grad_short * inv_root,
        grad_skip * inv_root,
        grad_first * inv_root,
        grad_second * inv_root,
        grad_third * inv_root,
    )

MESH = pl.DeviceIdType.MESH
f32 = jnp.float32
bf16 = jnp.bfloat16


def table_split(table):
    high = table.astype(ml_dtypes.bfloat16)
    return high, (table - high.astype(np.float32)).astype(ml_dtypes.bfloat16)


def split(value):
    high = value.astype(bf16)
    return high, (value - high.astype(f32)).astype(bf16)


def dot(left, right):
    return jnp.dot(left, right, preferred_element_type=f32)


def dot_full(left, right, contract=((1,), (0,))):
    return lax.dot_general(
        left, right, (contract, ((), ())), precision=highest, preferred_element_type=f32
    )


def low_lanes(shape):
    return lax.broadcasted_iota(jnp.int32, shape, len(shape) - 1) < shape[-1] // 2


def swap(value):
    return pltpu.roll(value, value.shape[-1] // 2, value.ndim - 1)


def greet(devices):
    barrier = pltpu.get_barrier_semaphore()
    for device in devices:
        pl.semaphore_signal(barrier, inc=1, device_id=device, device_id_type=MESH)
    pl.semaphore_wait(barrier, len(devices))


def pack_rows(number, query, key, cotangent, out):
    lanes = out.shape[-1]
    block = number // 2 * lanes
    key_part = key[:, block : block + lanes].astype(f32)
    grad_part = cotangent[:, block : block + lanes].astype(f32) * query[
        :, block : block + lanes
    ].astype(f32)
    low = low_lanes(key_part.shape)
    if number % 2 == 0:
        packed = jnp.where(low, key_part, swap(grad_part))
    else:
        packed = jnp.where(low, swap(key_part), grad_part)
    out[number] = packed


def one_less_exp(value):
    series = 1.0 - value / 9.0
    for order in range(8, 1, -1):
        series = 1.0 - value / order * series
    return jnp.where(value < 0.25, value * series, 1.0 - jnp.exp(-value))


def fused_kernel(
    count,
    groups,
    coefs,
    tokens,
    embed_table,
    short_conv,
    query,
    key,
    cotangent,
    decay_rate,
    first,
    second,
    weight_third,
    skip_gain,
    feats,
    twiddles,
    table_high,
    table_low,
    landed,
    small_landed,
    summed,
    staged,
    arrived,
    token_rows,
    token_landed,
    state,
    filters,
    windows,
    total,
    shape_total,
    value,
    embedded,
    gated,
    onehot,
    acts,
    filter_spec,
    shape_spec,
    pay,
    small,
    by_chan,
    held,
    by_seq,
    token_send,
    token_recv,
    out_send,
    out_recv,
    back_send,
    back_recv,
    small_send,
    small_recv,
    chan_send,
    chan_recv,
    scatter_send,
    scatter_recv,
    gather_send,
    gather_recv,
):
    me = lax.axis_index("seq")
    chan = lax.axis_index("chan")
    rows = key.shape[0]
    lanes = staged.shape[2]
    vocab = embed_table.shape[0]
    units = second.shape[0]
    feat = first.shape[0]
    length = count * rows
    share = vocab // count
    peers = [lax.rem(me + step, count) for step in range(1, count)]
    sources = [lax.rem(me + count - step, count) for step in range(1, count)]
    across = [lax.rem(chan + step, groups) for step in range(1, groups)]

    def post(source, target, send, recv, device):
        copy = pltpu.make_async_remote_copy(
            src_ref=source,
            dst_ref=target,
            send_sem=send,
            recv_sem=recv,
            device_id=device,
            device_id_type=MESH,
        )
        copy.start()
        return copy

    token_rows[...] = jnp.zeros_like(token_rows)
    token_rows[: tokens.shape[0]] = tokens[...].astype(f32)
    for number in range(count):
        pack_rows(number, query, key, cotangent, staged)
    greet([(peer, chan) for peer in peers] + [(me, group) for group in across])
    token_copies = [
        post(token_rows, token_landed.at[me], token_send.at[n], token_recv.at[n], (peer, chan))
        for n, peer in enumerate(peers)
    ]
    out_copies = [
        post(staged.at[peer], arrived.at[me], out_send.at[n], out_recv.at[n], (peer, chan))
        for n, peer in enumerate(peers)
    ]
    arrived[me] = staged[me]
    token_landed[me] = token_rows[...]

    columns = pl.ds(pl.multiple_of(me // 2 * lanes, lanes), lanes)
    parity = lax.rem(me, 2)

    def mine(array):
        lane = lax.broadcasted_iota(jnp.int32, array.shape, 1)
        return jnp.where(lane // (lanes // 2) == parity, array, swap(array))

    third = mine(weight_third[:, columns])
    table = mine(embed_table[:, columns].astype(f32)).astype(bf16)
    rate = mine(jnp.broadcast_to(decay_rate[:, columns], (8, lanes)))[:1]
    skip = mine(jnp.broadcast_to(skip_gain[:, columns], (8, lanes)))[:1]
    all_taps = [mine(jnp.broadcast_to(short_conv[j : j + 1, columns], (8, lanes))) for j in range(3)]
    taps = [tap[:1] for tap in all_taps]
    scale = jnp.sqrt(one_less_exp(2.0 * rate) / one_less_exp(2.0 * length * rate))
    low = low_lanes((rows, lanes))
    sign = jnp.where(low, 1.0, -1.0).astype(f32)

    pre_one = dot_full(first[...], feats[:feat], ((0,), (0,)))
    act_one = jnp.sin(pre_one)
    acts[0] = act_one
    acts[1] = jnp.cos(pre_one)
    pre_two = dot_full(second[...], act_one, ((0,), (0,)))
    acts[2] = jnp.sin(pre_two)
    acts[3] = jnp.cos(pre_two)
    row_ids = lax.broadcasted_iota(jnp.int32, (rows, lanes), 0).astype(f32)
    for block in range(count):
        act_rows = acts[2, :, block * rows : (block + 1) * rows].T
        window = scale * jnp.exp(-rate * (row_ids + float(block * rows)))
        windows[block] = window
        filters[block] = dot_full(act_rows, third) * window

    def spread(both):
        high, rest = split(both)
        product = (
            dot(table_high[...], high) + dot(table_high[...], rest) + dot(table_low[...], high)
        )
        return product[:rows], product[rows:]

    def forward(ref, lane):
        cos_t = twiddles[lane, 0]
        sin_t = twiddles[lane, 1]
        real = jnp.zeros((rows, lanes), f32)
        imag = jnp.zeros((rows, lanes), f32)
        for n in range(count):
            piece = ref[n]
            real = real + coefs[lane, n] * piece
            imag = imag - coefs[lane, count + n] * piece
        turned = jnp.concatenate(
            [real * cos_t + imag * sin_t, imag * cos_t - real * sin_t], axis=1
        )
        by_cos, by_sin = spread(turned)
        return (
            by_cos[:, :lanes] + by_sin[:, lanes:],
            by_cos[:, lanes:] - by_sin[:, :lanes],
        )

    def transform_filter(lane, carry):
        real, imag = forward(filters, lane)
        filter_spec[lane, 0] = real
        filter_spec[lane, 1] = imag * sign
        return carry

    lax.fori_loop(0, count + 1, transform_filter, 0)

    for copy in token_copies:
        copy.wait()
    embedded[:8] = jnp.zeros((8, lanes), f32)
    vocab_ids = lax.broadcasted_iota(jnp.int32, (vocab, lanes), 0).astype(f32)
    for block in range(count):
        for piece in range(rows // lanes):
            ids = token_landed[block, piece : piece + 1]
            matches = jnp.where(vocab_ids == ids, 1.0, 0.0)
            start = block * rows + piece * lanes
            onehot[:, start : start + lanes] = matches.astype(bf16)
            embedded[8 + start : 8 + start + lanes] = dot(matches.T.astype(bf16), table)
    for block in range(count):
        start = 8 + block * rows
        value[block] = (
            taps[0] * embedded[start : start + rows]
            + taps[1] * embedded[start - 1 : start - 1 + rows]
            + taps[2] * embedded[start - 2 : start - 2 + rows]
        )
    total[...] = jnp.zeros_like(total)
    shape_total[...] = jnp.zeros_like(shape_total)

    def gate(block):
        packed = arrived[block]
        state[block] = jnp.where(low, packed * value[block], packed)

    gate(me)
    for copy, source in zip(out_copies, sources):
        copy.wait()
        gate(source)

    def convolve(lane, carry):
        xr, xi = forward(state, lane)
        fr = filter_spec[lane, 0]
        fi = filter_spec[lane, 1]
        by_cos, by_sin = spread(jnp.concatenate([xr * fr - xi * fi, xr * fi + xi * fr], axis=1))
        zr = by_cos[:, :lanes] - by_sin[:, lanes:]
        zi = by_cos[:, lanes:] + by_sin[:, :lanes]
        cos_t = twiddles[lane, 0]
        sin_t = twiddles[lane, 1]
        ur = zr * cos_t - zi * sin_t
        ui = zr * sin_t + zi * cos_t
        for n in range(count):
            total[n] += coefs[lane, 2 * count + n] * ur - coefs[lane, 3 * count + n] * ui
        gr, gi = swap(xr), swap(xi)
        shape_spec[lane] = jnp.where(low, xr * gr + xi * gi, swap(xr * gi - xi * gr))
        return carry

    lax.fori_loop(0, count + 1, convolve, 0)

    def finish(block):
        summed_rows = total[block] + skip * state[block]
        total[block] = summed_rows
        return jnp.where(low, summed_rows, summed_rows * value[block])

    back_copies = []
    for n, peer in enumerate(peers):
        pay[peer] = finish(peer)
        back_copies.append(
            post(pay.at[peer], landed.at[me], back_send.at[n], back_recv.at[n], (peer, chan))
        )
    landed[me] = finish(me)

    def correlate(lane, carry):
        cos_t = twiddles[lane, 0]
        sin_t = twiddles[lane, 1]
        by_cos, by_sin = spread(shape_spec[lane])
        both = by_cos - sign * swap(by_sin)
        part_cos = both * jnp.where(low, cos_t, -sin_t)
        part_sin = both * jnp.where(low, sin_t, cos_t)
        for n in range(count):
            shape_total[n] += (
                coefs[lane, 2 * count + n] * part_cos - coefs[lane, 3 * count + n] * part_sin
            )
        return carry

    lax.fori_loop(0, count + 1, correlate, 0)
    inv_root = 1.0 / math.sqrt(length)
    third_sum = jnp.zeros((units, lanes), f32)
    third_low = jnp.where(low_lanes(third.shape), third, 0.0)
    for block in range(count):
        grad_rows = shape_total[block]
        grad_rows = (grad_rows + swap(grad_rows)) * windows[block]
        places = slice(block * rows, (block + 1) * rows)
        third_sum += dot_full(acts[2, :, places], grad_rows)
        acts[3, :, places] = dot_full(third_low, grad_rows, ((1,), (1,))) * acts[3, :, places]
    grad_pre_two = acts[3]
    grad_pre_one = dot_full(second[...], grad_pre_two) * acts[1]
    grad_both = jnp.concatenate([grad_pre_two, grad_pre_one], axis=0)
    from_act = dot_full(acts[0], grad_both, ((1,), (1,)))
    from_feats = dot_full(feats[...], grad_both, ((1,), (1,)))
    hidden = jnp.where(low_lanes(from_act.shape), from_act, from_feats) * inv_root
    strip = units // count
    for n in range(count):
        by_chan[chan, n] = hidden[n * strip : (n + 1) * strip]
    chan_copies = [
        post(by_chan.at[chan], by_chan.at[chan], chan_send.at[n], chan_recv.at[n], (me, group))
        for n, group in enumerate(across)
    ]

    gated[length:] = jnp.zeros((8, lanes), f32)
    short_sums = [jnp.zeros((1, lanes), f32) for _ in range(3)]
    skip_sum = jnp.zeros((1, lanes), f32)
    for block in range(count):
        start = block * rows
        grad_value = total[block] * swap(arrived[block])
        gated[start : start + rows] = grad_value
        for j in range(3):
            short_sums[j] += jnp.sum(
                grad_value * embedded[8 + start - j : 8 + start - j + rows], axis=0, keepdims=True
            )
        skip_sum += jnp.sum(state[block] * swap(state[block]), axis=0, keepdims=True)
    embed_sum = jnp.zeros((vocab, lanes), f32)
    for block in range(count):
        start = block * rows
        high, rest = split(
            taps[0] * gated[start : start + rows]
            + taps[1] * gated[start + 1 : start + 1 + rows]
            + taps[2] * gated[start + 2 : start + 2 + rows]
        )
        matches = onehot[:, start : start + rows]
        embed_sum += dot(matches, high) + dot(matches, rest)
    half = units // 2
    fold = jnp.where(low_lanes((half, lanes)), third_sum[:half], third_sum[half:])
    sums = jnp.concatenate([fold, *short_sums, skip_sum, jnp.zeros((4, lanes), f32)], axis=0)
    for block in range(count):
        top = embed_sum[block * share : block * share + share // 2]
        bottom = embed_sum[block * share + share // 2 : (block + 1) * share]
        folded = jnp.where(low_lanes(top.shape), swap(top), bottom)
        small[block] = jnp.concatenate([folded, sums], axis=0) * inv_root
    small_copies = [
        post(small.at[peer], small_landed.at[me], small_send.at[n], small_recv.at[n], (peer, chan))
        for n, peer in enumerate(peers)
    ]
    small_landed[me] = small[me]

    for copy in chan_copies:
        copy.wait()
    for n in range(count):
        strip_sum = by_chan[0, n]
        for group in range(1, groups):
            strip_sum = strip_sum + by_chan[group, n]
        held[n] = strip_sum
    scatter_copies = [
        post(held.at[peer], by_seq.at[me], scatter_send.at[n], scatter_recv.at[n], (peer, chan))
        for n, peer in enumerate(peers)
    ]
    by_seq[me] = held[me]
    for copy in scatter_copies:
        copy.wait()
    strip_sum = by_seq[0]
    for n in range(1, count):
        strip_sum = strip_sum + by_seq[n]
    summed[me] = strip_sum
    gather_copies = [
        post(summed.at[me], summed.at[me], gather_send.at[n], gather_recv.at[n], (peer, chan))
        for n, peer in enumerate(peers)
    ]
    for copy in back_copies + small_copies + gather_copies:
        copy.wait()


def finish_kernel(
    landed,
    small_landed,
    summed,
    query,
    cotangent,
    out,
    grad_query,
    grad_key,
    grad_embed,
    grad_short,
    grad_skip,
    grad_first,
    grad_second,
    grad_third,
):
    count, rows, lanes = landed.shape
    low = low_lanes((rows, lanes))
    share = grad_embed.shape[0]
    part = share // 2
    half = grad_third.shape[0] // 2
    for block in range(count // 2):
        columns = slice(block * lanes, (block + 1) * lanes)
        even, odd = landed[2 * block], landed[2 * block + 1]
        inner = jnp.where(low, even, swap(odd))
        out[:, columns] = (query[:, columns].astype(f32) * inner).astype(bf16)
        grad_query[:, columns] = (cotangent[:, columns].astype(f32) * inner).astype(bf16)
        grad_key[:, columns] = jnp.where(low, swap(even), odd).astype(bf16)
        even, odd = small_landed[2 * block], small_landed[2 * block + 1]
        left = low_lanes(even.shape)
        first_rows = jnp.where(left, even, swap(odd))
        last_rows = jnp.where(left, swap(even), odd)
        grad_embed[:part, columns] = first_rows[:part]
        grad_embed[part:, columns] = last_rows[:part]
        grad_third[:half, columns] = first_rows[part : part + half]
        grad_third[half:, columns] = last_rows[part : part + half]
        top = part + half
        grad_short[:, columns] = last_rows[top : top + 3]
        grad_skip[:, columns] = last_rows[top + 3 : top + 4]
    both = jnp.concatenate([summed[n] for n in range(count)], axis=0)
    units = grad_second.shape[0]
    grad_second[...] = both[:, :units]
    grad_first[...] = swap(both)[: grad_first.shape[0], :units]


def feature_table(length):
    positions = np.arange(length, dtype=np.int64)
    frequency = 2 ** np.arange(BANDS, dtype=np.int64) + 1
    phases = positions[:, None] * frequency[None, :] % length
    angles = phases.astype(np.float32) * np.float32(two_pi / length)
    ramp = positions.astype(np.float32)[:, None] / np.float32(length)
    return np.concatenate([ramp, np.cos(angles), np.sin(angles)], axis=1).T.astype(np.float32)


def fused_device(
    tokens,
    embed_table,
    short_conv,
    query_branch,
    key_branch,
    decay_rate,
    weight_first,
    weight_second,
    weight_third,
    skip_gain,
    cotangent,
):
    count = lax.axis_size("seq")
    groups = lax.axis_size("chan")
    seq_index = lax.axis_index("seq")
    rows, chan_width = query_branch.shape
    length = rows * count
    points = 2 * length
    vocab = embed_table.shape[0]
    hidden_units = weight_second.shape[0]
    feat = weight_first.shape[0]
    slice_width = chan_width // count
    lanes = 2 * slice_width
    share = vocab // count
    strip = hidden_units // count
    small_rows = share // 2 + hidden_units // 2 + 8
    vmem = pl.BlockSpec(memory_space=pltpu.VMEM)
    smem = pl.BlockSpec(memory_space=pltpu.SMEM)
    dma = pltpu.SemaphoreType.DMA

    depth = np.arange(rows)
    turns = np.arange(count + 1)
    angle = two_pi * (depth[:, None] * depth[None, :] % rows) / rows
    tables = np.concatenate([np.cos(angle), np.sin(angle)], axis=0).astype(np.float32)
    table_high, table_low = table_split(tables)
    twist = two_pi * (turns[:, None] * depth[None, :]) / points
    twiddles = np.stack([np.cos(twist), np.sin(twist)], axis=1).astype(np.float32)
    twiddles = np.broadcast_to(twiddles[..., None], (count + 1, 2, rows, lanes)).copy()
    small_angle = two_pi * (turns[:, None] * np.arange(count)[None, :] % (2 * count)) / (2 * count)
    weight = np.where((turns == 0) | (turns == count), 1.0, 2.0)[:, None] / points
    coefs = np.concatenate(
        [
            np.cos(small_angle),
            np.sin(small_angle),
            weight * np.cos(small_angle),
            weight * np.sin(small_angle),
        ],
        axis=1,
    ).astype(np.float32)
    feats = np.pad(feature_table(length), ((0, hidden_units - feat), (0, 0)))

    def whole(*shape):
        return jax.ShapeDtypeStruct(shape, f32)

    def buffer(*shape):
        return pltpu.VMEM(shape, f32)

    block_shape = (count, rows, lanes)
    landed, small_landed, summed = pl.pallas_call(
        functools.partial(fused_kernel, count, groups),
        out_shape=(
            whole(*block_shape),
            whole(count, small_rows, lanes),
            whole(count, strip, lanes),
        ),
        in_specs=[smem] + [vmem] * 15,
        out_specs=(vmem,) * 3,
        scratch_shapes=[
            buffer(*block_shape),
            buffer(*block_shape),
            buffer(8, lanes),
            buffer(count, 8, lanes),
            buffer(*block_shape),
            buffer(*block_shape),
            buffer(*block_shape),
            buffer(*block_shape),
            buffer(*block_shape),
            buffer(*block_shape),
            buffer(length + 8, lanes),
            buffer(length + 8, lanes),
            pltpu.VMEM((vocab, length), bf16),
            buffer(4, hidden_units, length),
            buffer(count + 1, 2, rows, lanes),
            buffer(count + 1, rows, lanes),
            buffer(*block_shape),
            buffer(count, small_rows, lanes),
            buffer(groups, count, strip, lanes),
            buffer(count, strip, lanes),
            buffer(count, strip, lanes),
        ]
        + [dma((count,))] * 8
        + [dma((groups,))] * 2
        + [dma((count,))] * 4,
        compiler_params=pltpu.CompilerParams(
            collective_id=0, has_side_effects=True, vmem_limit_bytes=52 * 2**20
        ),
        name="convolve_slices",
    )(
        jnp.asarray(coefs),
        tokens.reshape(rows // lanes, lanes),
        embed_table,
        short_conv,
        query_branch,
        key_branch,
        cotangent,
        decay_rate[None],
        weight_first,
        weight_second,
        weight_third,
        skip_gain[None],
        jnp.asarray(feats),
        jnp.asarray(twiddles),
        jnp.asarray(table_high),
        jnp.asarray(table_low),
    )
    half_out = jax.ShapeDtypeStruct((rows, chan_width), bf16)
    results = pl.pallas_call(
        finish_kernel,
        out_shape=(
            half_out,
            half_out,
            half_out,
            whole(share, chan_width),
            whole(3, chan_width),
            whole(1, chan_width),
            whole(feat, hidden_units),
            whole(hidden_units, hidden_units),
            whole(hidden_units, chan_width),
        ),
        in_specs=[vmem] * 5,
        out_specs=(vmem,) * 9,
        compiler_params=pltpu.CompilerParams(vmem_limit_bytes=32 * 2**20),
        name="finish_outputs",
    )(landed, small_landed, summed, query_branch, cotangent)
    return results[:5] + (results[5][0],) + results[6:]


def per_slice(*arrays):
    count = lax.axis_size("seq")
    rows, width = arrays[3].shape
    lanes = 2 * width // count
    units = arrays[7].shape[0]
    vocab = arrays[1].shape[0]
    tiled = lanes % 128 == 0 and rows % lanes == 0 and rows <= 8 * lanes
    even = count % 2 == 0 and 2 * units == lanes and units % (8 * count) == 0
    body = fused_device if tiled and even and vocab % (16 * count) == 0 else per_device
    return body(*arrays)


def solution(mesh):
    in_specs = (
        P("seq"),
        P(None, "chan"),
        P(None, "chan"),
        P("seq", "chan"),
        P("seq", "chan"),
        P("chan"),
        P(),
        P(),
        P(None, "chan"),
        P("chan"),
        P("seq", "chan"),
    )
    out_specs = (
        P("seq", "chan"),
        P("seq", "chan"),
        P("seq", "chan"),
        P("seq", "chan"),
        P(None, "chan"),
        P("chan"),
        P(),
        P(),
        P(None, "chan"),
    )
    return jax.shard_map(
        per_slice, mesh=mesh, in_specs=in_specs, out_specs=out_specs, check_vma=False
    )
```

```python
import functools
import math

import jax
import jax.numpy as jnp
import numpy as np
from jax import lax
from jax.experimental import pallas as pl
from jax.experimental.pallas import tpu as pltpu
from jax.sharding import PartitionSpec as P

BANDS = 16


highest = lax.Precision.HIGHEST
two_pi = 2.0 * math.pi


def from_behind(value, axis, steps):
    count = lax.axis_size(axis)
    leading, last = (max(0, -steps), min(count, count - steps))
    return lax.ppermute(value, axis, [(source, source + steps) for source in range(leading, last)])


def features(positions, length):
    frequency = 2 ** jnp.arange(BANDS, dtype=jnp.int32) + 1
    phases = positions[:, None] * frequency[None, :] % length
    angles = phases.astype(jnp.float32) * (two_pi / length)
    ramp_col = positions.astype(jnp.float32)[:, None] / length
    return jnp.concatenate([ramp_col, jnp.cos(angles), jnp.sin(angles)], axis=1)


def filter_forward(positions, length, weight_first, weight_second, weight_third, decay_rate):
    embedding = features(positions, length)
    pre_one = jnp.dot(
        embedding, weight_first, precision=highest, preferred_element_type=jnp.float32
    )
    act_one = jnp.sin(pre_one)
    pre_two = jnp.dot(act_one, weight_second, precision=highest, preferred_element_type=jnp.float32)
    act_two = jnp.sin(pre_two)
    shaped = jnp.dot(act_two, weight_third, precision=highest, preferred_element_type=jnp.float32)
    scaling = jnp.sqrt(jnp.expm1(-2.0 * decay_rate) / jnp.expm1(-2.0 * length * decay_rate))
    window = scaling[None, :] * jnp.exp(
        -decay_rate[None, :] * positions.astype(jnp.float32)[:, None]
    )
    return (shaped * window, (window, embedding, pre_one, act_one, pre_two, act_two))


def filter_head(grad_filter, saved_acts, weight_third):
    window, embedding, pre_one, act_one, pre_two, act_two = saved_acts
    grad_shaped = grad_filter * window
    grad_third = jnp.dot(
        act_two.T, grad_shaped, precision=highest, preferred_element_type=jnp.float32
    )
    grad_act_two = jnp.dot(
        grad_shaped, weight_third.T, precision=highest, preferred_element_type=jnp.float32
    )
    return (grad_third, grad_act_two)


def filter_tail(grad_act_two, saved_acts, weight_second):
    window, embedding, pre_one, act_one, pre_two, act_two = saved_acts
    grad_pre_two = grad_act_two * jnp.cos(pre_two)
    grad_second = jnp.dot(
        act_one.T, grad_pre_two, precision=highest, preferred_element_type=jnp.float32
    )
    grad_act_one = jnp.dot(
        grad_pre_two, weight_second.T, precision=highest, preferred_element_type=jnp.float32
    )
    grad_pre_one = grad_act_one * jnp.cos(pre_one)
    grad_first = jnp.dot(
        embedding.T, grad_pre_one, precision=highest, preferred_element_type=jnp.float32
    )
    return (grad_first, grad_second)


def rotation(first_index, second_index, modulus):
    phases = first_index * second_index % modulus
    angles = phases.astype(jnp.float32) * (two_pi / modulus)
    return (jnp.cos(angles), jnp.sin(angles))


def lane_forward(lane_rows, seq_count, points):
    width, length = lane_rows.shape
    depth_rows = length // seq_count
    blocks = lane_rows.reshape(width, seq_count, depth_rows)
    source_index = jnp.arange(seq_count, dtype=jnp.int32)
    lane_index = jnp.arange(2 * seq_count, dtype=jnp.int32)
    cosine_part, sine_part = rotation(lane_index[:, None], source_index[None, :], 2 * seq_count)
    small_table = jnp.concatenate([cosine_part, -sine_part], axis=0)
    product = jnp.einsum("kn,cnm->ckm", small_table, blocks, precision=highest)
    real_part = product[:, : 2 * seq_count]
    imag_part = product[:, 2 * seq_count :]
    cos_twist, sin_twist = rotation(
        lane_index[:, None], jnp.arange(depth_rows, dtype=jnp.int32)[None, :], points
    )
    turned = jnp.stack(
        [
            real_part * cos_twist + imag_part * sin_twist,
            imag_part * cos_twist - real_part * sin_twist,
        ]
    )
    grid_index = jnp.arange(depth_rows, dtype=jnp.int32)
    cos_block, sin_block = rotation(grid_index[:, None], grid_index[None, :], depth_rows)
    tables = jnp.concatenate([cos_block, sin_block], axis=1)
    both_parts = jnp.einsum("rckm,mj->rckj", turned, tables, precision=highest)
    return jnp.stack(
        [
            both_parts[0, :, :, :depth_rows] + both_parts[1, :, :, depth_rows:],
            both_parts[1, :, :, :depth_rows] - both_parts[0, :, :, depth_rows:],
        ]
    )


def lane_inverse(spectrum, seq_count, points):
    width = spectrum.shape[1]
    depth_rows = spectrum.shape[3]
    grid_index = jnp.arange(depth_rows, dtype=jnp.int32)
    cos_block, sin_block = rotation(grid_index[:, None], grid_index[None, :], depth_rows)
    tables = jnp.concatenate([cos_block, sin_block], axis=1)
    both_parts = jnp.einsum("rckm,mj->rckj", spectrum, tables, precision=highest)
    real_part = both_parts[0, :, :, :depth_rows] - both_parts[1, :, :, depth_rows:]
    imag_part = both_parts[1, :, :, :depth_rows] + both_parts[0, :, :, depth_rows:]
    lane_index = jnp.arange(2 * seq_count, dtype=jnp.int32)
    cos_twist, sin_twist = rotation(lane_index[:, None], grid_index[None, :], points)
    turned = jnp.stack(
        [
            real_part * cos_twist - imag_part * sin_twist,
            imag_part * cos_twist + real_part * sin_twist,
        ]
    )
    source_index = jnp.arange(seq_count, dtype=jnp.int32)
    cosine_part, sine_part = rotation(source_index[:, None], lane_index[None, :], 2 * seq_count)
    back_table = jnp.stack([cosine_part, -sine_part]) / points
    result_rows = jnp.einsum("rnk,rckm->cnm", back_table, turned, precision=highest)
    return result_rows.reshape(width, seq_count * depth_rows)


def pointwise(spectra):
    keyed_spec, filter_spec, grad_spec = spectra
    conv_spec = jnp.stack(
        [
            keyed_spec[0] * filter_spec[0] - keyed_spec[1] * filter_spec[1],
            keyed_spec[0] * filter_spec[1] + keyed_spec[1] * filter_spec[0],
        ]
    )
    back_spec = jnp.stack(
        [
            filter_spec[0] * grad_spec[0] + filter_spec[1] * grad_spec[1],
            filter_spec[0] * grad_spec[1] - filter_spec[1] * grad_spec[0],
        ]
    )
    shape_spec = jnp.stack(
        [
            keyed_spec[0] * grad_spec[0] + keyed_spec[1] * grad_spec[1],
            keyed_spec[0] * grad_spec[1] - keyed_spec[1] * grad_spec[0],
        ]
    )
    return (conv_spec, back_spec, shape_spec)


def per_device(
    tokens,
    embed_table,
    short_conv,
    query_branch,
    key_branch,
    decay_rate,
    weight_first,
    weight_second,
    weight_third,
    skip_gain,
    cotangent,
):
    seq_count = lax.axis_size("seq")
    seq_index = lax.axis_index("seq")
    row_count = query_branch.shape[0]
    chan_width = query_branch.shape[1]
    length = row_count * seq_count
    points = 2 * length
    inv_root = 1.0 / math.sqrt(length)
    vocab_size = embed_table.shape[0]
    earlier = from_behind(tokens[row_count - 2 :], "seq", 1)
    window_ids = jnp.concatenate([earlier, tokens])
    row_start = seq_index * row_count
    window_pos = row_start + jnp.arange(row_count + 2, dtype=jnp.int32) - 2
    present = window_pos >= 0
    vocab_ids = jnp.arange(vocab_size, dtype=jnp.int32)
    lookup = ((window_ids[:, None] == vocab_ids[None, :]) & present[:, None]).astype(jnp.bfloat16)
    embedded = jnp.dot(lookup, embed_table, preferred_element_type=jnp.float32)
    value_branch = (
        short_conv[0] * embedded[2:]
        + short_conv[1] * embedded[1:-1]
        + short_conv[2] * embedded[:-2]
    )
    key_rows = key_branch.astype(jnp.float32)
    keyed_value = key_rows * value_branch
    query_rows = query_branch.astype(jnp.float32)
    grad_out = cotangent.astype(jnp.float32)
    grad_z = grad_out * query_rows
    slice_width = chan_width // seq_count
    chan_start = seq_index * slice_width
    third_slice = lax.dynamic_slice_in_dim(weight_third, chan_start, slice_width, 1)
    rate_slice = lax.dynamic_slice_in_dim(decay_rate, chan_start, slice_width, 0)
    all_positions = jnp.arange(length, dtype=jnp.int32)
    filter_full, tail_acts = filter_forward(
        all_positions, length, weight_first, weight_second, third_slice, rate_slice
    )
    keyed_lanes, grad_lanes = (
        lax.all_to_all(keyed_value.T, "seq", split_axis=0, concat_axis=1, tiled=True),
        lax.all_to_all(grad_z.T, "seq", split_axis=0, concat_axis=1, tiled=True),
    )
    spectra = (
        lane_forward(keyed_lanes, seq_count, points),
        lane_forward(filter_full.T, seq_count, points),
        lane_forward(grad_lanes, seq_count, points),
    )
    conv_spec, back_spec, shape_spec = pointwise(spectra)
    conv_lanes = lane_inverse(conv_spec, seq_count, points)
    back_lanes = lane_inverse(back_spec, seq_count, points)
    filter_lanes = lane_inverse(shape_spec, seq_count, points)
    conv_rows, back_rows = (
        lax.all_to_all(conv_lanes, "seq", split_axis=1, concat_axis=0, tiled=True),
        lax.all_to_all(back_lanes, "seq", split_axis=1, concat_axis=0, tiled=True),
    )
    convolved = conv_rows.T
    back_keyed = back_rows.T
    third_small, act_two_part = filter_head(filter_lanes.T, tail_acts, third_slice)
    third_part = lax.dynamic_update_slice(
        jnp.zeros((third_small.shape[0], chan_width), jnp.float32),
        third_small,
        (jnp.zeros((), jnp.int32), chan_start),
    )
    inner_sum = convolved + skip_gain * keyed_value
    operator_out = (query_rows * inner_sum).astype(jnp.bfloat16)
    grad_query = (grad_out * inner_sum).astype(jnp.bfloat16)
    grad_keyed = back_keyed + skip_gain * grad_z
    grad_key = (grad_keyed * value_branch).astype(jnp.bfloat16)
    grad_value = grad_keyed * key_rows
    short_part = jnp.stack(
        [
            jnp.sum(grad_value * embedded[2 - offset : 2 - offset + row_count], axis=0)
            for offset in range(3)
        ]
    )
    skip_part = jnp.sum(grad_z * keyed_value, axis=0)
    ids_stacked = jnp.concatenate([window_ids[2:], window_ids[1:-1], window_ids[:-2]])
    live_stacked = jnp.concatenate([present[2:], present[1:-1], present[:-2]])
    weighted = jnp.concatenate([short_conv[offset] * grad_value for offset in range(3)], axis=0)
    vocab_rows = jnp.arange(vocab_size // seq_count * lax.axis_size("seq"), dtype=jnp.int32)
    matches = ((vocab_rows[:, None] == ids_stacked[None, :]) & live_stacked[None, :]).astype(
        jnp.float32
    )
    grad_embed = (
        lax.psum_scatter(
            jnp.dot(matches, weighted, precision=highest, preferred_element_type=jnp.float32),
            "seq",
            scatter_dimension=0,
            tiled=True,
        )
        * inv_root
    )
    grad_act_two = lax.psum(act_two_part, "chan")
    first_part, second_part = filter_tail(grad_act_two, tail_acts, weight_second)
    grad_short, grad_skip, grad_third, grad_first, grad_second = lax.psum(
        (short_part, skip_part, third_part, first_part, second_part), "seq"
    )
    return (
        operator_out,
        grad_query,
        grad_key,
        grad_embed,
        grad_short * inv_root,
        grad_skip * inv_root,
        grad_first * inv_root,
        grad_second * inv_root,
        grad_third * inv_root,
    )

MESH = pl.DeviceIdType.MESH
f32 = jnp.float32
bf16 = jnp.bfloat16


def split(value):
    high = value.astype(bf16)
    return high, (value - high.astype(f32)).astype(bf16)


def dot(left, right):
    return jnp.dot(left, right, preferred_element_type=f32)


def dot_full(left, right, contract=((1,), (0,))):
    return lax.dot_general(
        left, right, (contract, ((), ())), precision=highest, preferred_element_type=f32
    )


def low_lanes(shape):
    return lax.broadcasted_iota(jnp.int32, shape, len(shape) - 1) < shape[-1] // 2


def swap(value):
    return pltpu.roll(value, value.shape[-1] // 2, value.ndim - 1)


def greet(devices):
    barrier = pltpu.get_barrier_semaphore()
    for device in devices:
        pl.semaphore_signal(barrier, inc=1, device_id=device, device_id_type=MESH)
    pl.semaphore_wait(barrier, len(devices))


def pack_rows(number, query, key, cotangent, out):
    lanes = out.shape[-1]
    block = number // 2 * lanes
    key_part = key[:, block : block + lanes].astype(f32)
    grad_part = cotangent[:, block : block + lanes].astype(f32) * query[
        :, block : block + lanes
    ].astype(f32)
    low = low_lanes(key_part.shape)
    if number % 2 == 0:
        packed = jnp.where(low, key_part, swap(grad_part))
    else:
        packed = jnp.where(low, swap(key_part), grad_part)
    out[number] = packed


def one_less_exp(value):
    series = 1.0 - value / 9.0
    for order in range(8, 1, -1):
        series = 1.0 - value / order * series
    return jnp.where(value < 0.25, value * series, 1.0 - jnp.exp(-value))


def fused_kernel(
    count,
    groups,
    coefs,
    tokens,
    embed_table,
    short_conv,
    query,
    key,
    cotangent,
    decay_rate,
    first,
    second,
    weight_third,
    skip_gain,
    feats,
    twiddles,
    tables,
    landed,
    small_landed,
    summed,
    held_inputs,
    input_sems,
    table_high,
    table_low,
    staged,
    arrived,
    token_rows,
    token_landed,
    state,
    filters,
    windows,
    total,
    shape_total,
    value,
    embedded,
    gated,
    onehot,
    acts,
    filter_spec,
    shape_spec,
    pay,
    small,
    by_chan,
    held,
    by_seq,
    token_send,
    token_recv,
    out_send,
    out_recv,
    back_send,
    back_recv,
    small_send,
    small_recv,
    chan_send,
    chan_recv,
    scatter_send,
    scatter_recv,
    gather_send,
    gather_recv,
):
    me = lax.axis_index("seq")
    chan = lax.axis_index("chan")
    sources = (
        (key, query, cotangent, tokens)
        + (first, second, feats, embed_table, short_conv, decay_rate, weight_third)
        + (skip_gain, twiddles, tables)
    )
    loads = [
        pltpu.make_async_copy(source, target, input_sems.at[n])
        for n, (source, target) in enumerate(zip(sources, held_inputs))
    ]
    for load in loads:
        load.start()
    key, query, cotangent, tokens, first, second, feats = held_inputs[:7]
    embed_table, short_conv, decay_rate, weight_third = held_inputs[7:11]
    skip_gain, twiddles, tables = held_inputs[11:]
    rows = key.shape[0]
    lanes = staged.shape[2]
    vocab = embed_table.shape[0]
    units = second.shape[0]
    feat = first.shape[0]
    length = count * rows
    share = vocab // count
    peers = [lax.rem(me + step, count) for step in range(1, count)]
    sources = [lax.rem(me + count - step, count) for step in range(1, count)]
    across = [lax.rem(chan + step, groups) for step in range(1, groups)]

    def post(source, target, send, recv, device):
        copy = pltpu.make_async_remote_copy(
            src_ref=source,
            dst_ref=target,
            send_sem=send,
            recv_sem=recv,
            device_id=device,
            device_id_type=MESH,
        )
        copy.start()
        return copy

    for load in loads[:4]:
        load.wait()
    token_rows[...] = jnp.zeros_like(token_rows)
    token_rows[: tokens.shape[0]] = tokens[...].astype(f32)
    for number in range(count):
        pack_rows(number, query, key, cotangent, staged)
    greet([(peer, chan) for peer in peers] + [(me, group) for group in across])
    token_copies = [
        post(token_rows, token_landed.at[me], token_send.at[n], token_recv.at[n], (peer, chan))
        for n, peer in enumerate(peers)
    ]
    out_copies = [
        post(staged.at[peer], arrived.at[me], out_send.at[n], out_recv.at[n], (peer, chan))
        for n, peer in enumerate(peers)
    ]
    arrived[me] = staged[me]
    token_landed[me] = token_rows[...]

    for load in loads[4:]:
        load.wait()
    table_high[...], table_low[...] = split(tables[...])

    columns = pl.ds(pl.multiple_of(me // 2 * lanes, lanes), lanes)
    parity = lax.rem(me, 2)

    def mine(array):
        lane = lax.broadcasted_iota(jnp.int32, array.shape, 1)
        return jnp.where(lane // (lanes // 2) == parity, array, swap(array))

    third = mine(weight_third[:, columns])
    table = mine(embed_table[:, columns].astype(f32)).astype(bf16)
    rate = mine(jnp.broadcast_to(decay_rate[:, columns], (8, lanes)))[:1]
    skip = mine(jnp.broadcast_to(skip_gain[:, columns], (8, lanes)))[:1]
    all_taps = [mine(jnp.broadcast_to(short_conv[j : j + 1, columns], (8, lanes))) for j in range(3)]
    taps = [tap[:1] for tap in all_taps]
    scale = jnp.sqrt(one_less_exp(2.0 * rate) / one_less_exp(2.0 * length * rate))
    low = low_lanes((rows, lanes))
    sign = jnp.where(low, 1.0, -1.0).astype(f32)

    pre_one = dot_full(first[...], feats[:feat], ((0,), (0,)))
    act_one = jnp.sin(pre_one)
    acts[0] = act_one
    acts[1] = jnp.cos(pre_one)
    pre_two = dot_full(second[...], act_one, ((0,), (0,)))
    acts[2] = jnp.sin(pre_two)
    acts[3] = jnp.cos(pre_two)
    row_ids = lax.broadcasted_iota(jnp.int32, (rows, lanes), 0).astype(f32)
    for block in range(count):
        act_rows = acts[2, :, block * rows : (block + 1) * rows].T
        window = scale * jnp.exp(-rate * (row_ids + float(block * rows)))
        windows[block] = window
        filters[block] = dot_full(act_rows, third) * window

    def spread(both):
        high, rest = split(both)
        product = (
            dot(table_high[...], high) + dot(table_high[...], rest) + dot(table_low[...], high)
        )
        return product[:rows], product[rows:]

    def forward(ref, lane):
        cos_t = twiddles[lane, 0]
        sin_t = twiddles[lane, 1]
        real = jnp.zeros((rows, lanes), f32)
        imag = jnp.zeros((rows, lanes), f32)
        for n in range(count):
            piece = ref[n]
            real = real + coefs[lane, n] * piece
            imag = imag - coefs[lane, count + n] * piece
        turned = jnp.concatenate(
            [real * cos_t + imag * sin_t, imag * cos_t - real * sin_t], axis=1
        )
        by_cos, by_sin = spread(turned)
        return (
            by_cos[:, :lanes] + by_sin[:, lanes:],
            by_cos[:, lanes:] - by_sin[:, :lanes],
        )

    def transform_filter(lane, carry):
        real, imag = forward(filters, lane)
        filter_spec[lane, 0] = real
        filter_spec[lane, 1] = imag * sign
        return carry

    lax.fori_loop(0, count + 1, transform_filter, 0)

    for copy in token_copies:
        copy.wait()
    embedded[:8] = jnp.zeros((8, lanes), f32)
    vocab_ids = lax.broadcasted_iota(jnp.int32, (vocab, lanes), 0).astype(f32)
    for block in range(count):
        for piece in range(rows // lanes):
            ids = token_landed[block, piece : piece + 1]
            matches = jnp.where(vocab_ids == ids, 1.0, 0.0)
            start = block * rows + piece * lanes
            onehot[:, start : start + lanes] = matches.astype(bf16)
            embedded[8 + start : 8 + start + lanes] = dot(matches.T.astype(bf16), table)
    for block in range(count):
        start = 8 + block * rows
        value[block] = (
            taps[0] * embedded[start : start + rows]
            + taps[1] * embedded[start - 1 : start - 1 + rows]
            + taps[2] * embedded[start - 2 : start - 2 + rows]
        )
    total[...] = jnp.zeros_like(total)
    shape_total[...] = jnp.zeros_like(shape_total)

    def gate(block):
        packed = arrived[block]
        state[block] = jnp.where(low, packed * value[block], packed)

    gate(me)
    for copy, source in zip(out_copies, sources):
        copy.wait()
        gate(source)

    def convolve(lane, carry):
        xr, xi = forward(state, lane)
        fr = filter_spec[lane, 0]
        fi = filter_spec[lane, 1]
        by_cos, by_sin = spread(jnp.concatenate([xr * fr - xi * fi, xr * fi + xi * fr], axis=1))
        zr = by_cos[:, :lanes] - by_sin[:, lanes:]
        zi = by_cos[:, lanes:] + by_sin[:, :lanes]
        cos_t = twiddles[lane, 0]
        sin_t = twiddles[lane, 1]
        ur = zr * cos_t - zi * sin_t
        ui = zr * sin_t + zi * cos_t
        for n in range(count):
            total[n] += coefs[lane, 2 * count + n] * ur - coefs[lane, 3 * count + n] * ui
        gr, gi = swap(xr), swap(xi)
        shape_spec[lane] = jnp.where(low, xr * gr + xi * gi, swap(xr * gi - xi * gr))
        return carry

    lax.fori_loop(0, count + 1, convolve, 0)

    def finish(block):
        summed_rows = total[block] + skip * state[block]
        total[block] = summed_rows
        return jnp.where(low, summed_rows, summed_rows * value[block])

    back_copies = []
    for n, peer in enumerate(peers):
        pay[peer] = finish(peer)
        back_copies.append(
            post(pay.at[peer], landed.at[me], back_send.at[n], back_recv.at[n], (peer, chan))
        )
    landed[me] = finish(me)

    def correlate(lane, carry):
        cos_t = twiddles[lane, 0]
        sin_t = twiddles[lane, 1]
        by_cos, by_sin = spread(shape_spec[lane])
        both = by_cos - sign * swap(by_sin)
        part_cos = both * jnp.where(low, cos_t, -sin_t)
        part_sin = both * jnp.where(low, sin_t, cos_t)
        for n in range(count):
            shape_total[n] += (
                coefs[lane, 2 * count + n] * part_cos - coefs[lane, 3 * count + n] * part_sin
            )
        return carry

    lax.fori_loop(0, count + 1, correlate, 0)
    inv_root = 1.0 / math.sqrt(length)
    third_sum = jnp.zeros((units, lanes), f32)
    third_low = jnp.where(low_lanes(third.shape), third, 0.0)
    for block in range(count):
        grad_rows = shape_total[block]
        grad_rows = (grad_rows + swap(grad_rows)) * windows[block]
        places = slice(block * rows, (block + 1) * rows)
        third_sum += dot_full(acts[2, :, places], grad_rows)
        acts[3, :, places] = dot_full(third_low, grad_rows, ((1,), (1,))) * acts[3, :, places]
    grad_pre_two = acts[3]
    grad_pre_one = dot_full(second[...], grad_pre_two) * acts[1]
    grad_both = jnp.concatenate([grad_pre_two, grad_pre_one], axis=0)
    from_act = dot_full(acts[0], grad_both, ((1,), (1,)))
    from_feats = dot_full(feats[...], grad_both, ((1,), (1,)))
    hidden = jnp.where(low_lanes(from_act.shape), from_act, from_feats) * inv_root
    strip = units // count
    for n in range(count):
        by_chan[chan, n] = hidden[n * strip : (n + 1) * strip]
    chan_copies = [
        post(by_chan.at[chan], by_chan.at[chan], chan_send.at[n], chan_recv.at[n], (me, group))
        for n, group in enumerate(across)
    ]

    gated[length:] = jnp.zeros((8, lanes), f32)
    short_sums = [jnp.zeros((1, lanes), f32) for _ in range(3)]
    skip_sum = jnp.zeros((1, lanes), f32)
    for block in range(count):
        start = block * rows
        grad_value = total[block] * swap(arrived[block])
        gated[start : start + rows] = grad_value
        for j in range(3):
            short_sums[j] += jnp.sum(
                grad_value * embedded[8 + start - j : 8 + start - j + rows], axis=0, keepdims=True
            )
        skip_sum += jnp.sum(state[block] * swap(state[block]), axis=0, keepdims=True)
    embed_sum = jnp.zeros((vocab, lanes), f32)
    for block in range(count):
        start = block * rows
        high, rest = split(
            taps[0] * gated[start : start + rows]
            + taps[1] * gated[start + 1 : start + 1 + rows]
            + taps[2] * gated[start + 2 : start + 2 + rows]
        )
        matches = onehot[:, start : start + rows]
        embed_sum += dot(matches, high) + dot(matches, rest)
    half = units // 2
    fold = jnp.where(low_lanes((half, lanes)), third_sum[:half], third_sum[half:])
    sums = jnp.concatenate([fold, *short_sums, skip_sum, jnp.zeros((4, lanes), f32)], axis=0)
    for block in range(count):
        top = embed_sum[block * share : block * share + share // 2]
        bottom = embed_sum[block * share + share // 2 : (block + 1) * share]
        folded = jnp.where(low_lanes(top.shape), swap(top), bottom)
        small[block] = jnp.concatenate([folded, sums], axis=0) * inv_root
    small_copies = [
        post(small.at[peer], small_landed.at[me], small_send.at[n], small_recv.at[n], (peer, chan))
        for n, peer in enumerate(peers)
    ]
    small_landed[me] = small[me]

    for copy in chan_copies:
        copy.wait()
    for n in range(count):
        strip_sum = by_chan[0, n]
        for group in range(1, groups):
            strip_sum = strip_sum + by_chan[group, n]
        held[n] = strip_sum
    scatter_copies = [
        post(held.at[peer], by_seq.at[me], scatter_send.at[n], scatter_recv.at[n], (peer, chan))
        for n, peer in enumerate(peers)
    ]
    by_seq[me] = held[me]
    for copy in scatter_copies:
        copy.wait()
    strip_sum = by_seq[0]
    for n in range(1, count):
        strip_sum = strip_sum + by_seq[n]
    summed[me] = strip_sum
    gather_copies = [
        post(summed.at[me], summed.at[me], gather_send.at[n], gather_recv.at[n], (peer, chan))
        for n, peer in enumerate(peers)
    ]
    for copy in back_copies + small_copies + gather_copies:
        copy.wait()


def finish_kernel(
    landed,
    small_landed,
    summed,
    query,
    cotangent,
    out,
    grad_query,
    grad_key,
    grad_embed,
    grad_short,
    grad_skip,
    grad_first,
    grad_second,
    grad_third,
):
    count, rows, lanes = landed.shape
    low = low_lanes((rows, lanes))
    share = grad_embed.shape[0]
    part = share // 2
    half = grad_third.shape[0] // 2
    for block in range(count // 2):
        columns = slice(block * lanes, (block + 1) * lanes)
        even, odd = landed[2 * block], landed[2 * block + 1]
        inner = jnp.where(low, even, swap(odd))
        out[:, columns] = (query[:, columns].astype(f32) * inner).astype(bf16)
        grad_query[:, columns] = (cotangent[:, columns].astype(f32) * inner).astype(bf16)
        grad_key[:, columns] = jnp.where(low, swap(even), odd).astype(bf16)
        even, odd = small_landed[2 * block], small_landed[2 * block + 1]
        left = low_lanes(even.shape)
        first_rows = jnp.where(left, even, swap(odd))
        last_rows = jnp.where(left, swap(even), odd)
        grad_embed[:part, columns] = first_rows[:part]
        grad_embed[part:, columns] = last_rows[:part]
        grad_third[:half, columns] = first_rows[part : part + half]
        grad_third[half:, columns] = last_rows[part : part + half]
        top = part + half
        grad_short[:, columns] = last_rows[top : top + 3]
        grad_skip[:, columns] = last_rows[top + 3 : top + 4]
    both = jnp.concatenate([summed[n] for n in range(count)], axis=0)
    units = grad_second.shape[0]
    grad_second[...] = both[:, :units]
    grad_first[...] = swap(both)[: grad_first.shape[0], :units]


def feature_table(length):
    positions = np.arange(length, dtype=np.int64)
    frequency = 2 ** np.arange(BANDS, dtype=np.int64) + 1
    phases = positions[:, None] * frequency[None, :] % length
    angles = phases.astype(np.float32) * np.float32(two_pi / length)
    ramp = positions.astype(np.float32)[:, None] / np.float32(length)
    return np.concatenate([ramp, np.cos(angles), np.sin(angles)], axis=1).T.astype(np.float32)


def fused_device(
    tokens,
    embed_table,
    short_conv,
    query_branch,
    key_branch,
    decay_rate,
    weight_first,
    weight_second,
    weight_third,
    skip_gain,
    cotangent,
):
    count = lax.axis_size("seq")
    groups = lax.axis_size("chan")
    seq_index = lax.axis_index("seq")
    rows, chan_width = query_branch.shape
    length = rows * count
    points = 2 * length
    vocab = embed_table.shape[0]
    hidden_units = weight_second.shape[0]
    feat = weight_first.shape[0]
    slice_width = chan_width // count
    lanes = 2 * slice_width
    share = vocab // count
    strip = hidden_units // count
    small_rows = share // 2 + hidden_units // 2 + 8
    vmem = pl.BlockSpec(memory_space=pltpu.VMEM)
    smem = pl.BlockSpec(memory_space=pltpu.SMEM)
    dma = pltpu.SemaphoreType.DMA

    depth = np.arange(rows)
    turns = np.arange(count + 1)
    angle = two_pi * (depth[:, None] * depth[None, :] % rows) / rows
    tables = np.concatenate([np.cos(angle), np.sin(angle)], axis=0).astype(np.float32)
    twist = two_pi * (turns[:, None] * depth[None, :]) / points
    twiddles = np.stack([np.cos(twist), np.sin(twist)], axis=1).astype(np.float32)
    twiddles = np.broadcast_to(twiddles[..., None], (count + 1, 2, rows, lanes)).copy()
    small_angle = two_pi * (turns[:, None] * np.arange(count)[None, :] % (2 * count)) / (2 * count)
    weight = np.where((turns == 0) | (turns == count), 1.0, 2.0)[:, None] / points
    coefs = np.concatenate(
        [
            np.cos(small_angle),
            np.sin(small_angle),
            weight * np.cos(small_angle),
            weight * np.sin(small_angle),
        ],
        axis=1,
    ).astype(np.float32)
    feats = np.pad(feature_table(length), ((0, hidden_units - feat), (0, 0)))

    def whole(*shape):
        return jax.ShapeDtypeStruct(shape, f32)

    def buffer(*shape):
        return pltpu.VMEM(shape, f32)

    block_shape = (count, rows, lanes)
    operands = (
        tokens.reshape(rows // lanes, lanes),
        embed_table,
        short_conv,
        query_branch,
        key_branch,
        cotangent,
        decay_rate[None],
        weight_first,
        weight_second,
        weight_third,
        skip_gain[None],
        jnp.asarray(feats),
        jnp.asarray(twiddles),
        jnp.asarray(tables),
    )
    load_order = (4, 3, 5, 0, 7, 8, 11, 1, 2, 6, 9, 10, 12, 13)
    landed, small_landed, summed = pl.pallas_call(
        functools.partial(fused_kernel, count, groups),
        out_shape=(
            whole(*block_shape),
            whole(count, small_rows, lanes),
            whole(count, strip, lanes),
        ),
        in_specs=[smem] + [pl.BlockSpec(memory_space=pltpu.HBM)] * 14,
        out_specs=(vmem,) * 3,
        scratch_shapes=[
            [pltpu.VMEM(operands[n].shape, operands[n].dtype) for n in load_order],
            dma((len(load_order),)),
            pltpu.VMEM(tables.shape, bf16),
            pltpu.VMEM(tables.shape, bf16),
            buffer(*block_shape),
            buffer(*block_shape),
            buffer(8, lanes),
            buffer(count, 8, lanes),
            buffer(*block_shape),
            buffer(*block_shape),
            buffer(*block_shape),
            buffer(*block_shape),
            buffer(*block_shape),
            buffer(*block_shape),
            buffer(length + 8, lanes),
            buffer(length + 8, lanes),
            pltpu.VMEM((vocab, length), bf16),
            buffer(4, hidden_units, length),
            buffer(count + 1, 2, rows, lanes),
            buffer(count + 1, rows, lanes),
            buffer(*block_shape),
            buffer(count, small_rows, lanes),
            buffer(groups, count, strip, lanes),
            buffer(count, strip, lanes),
            buffer(count, strip, lanes),
        ]
        + [dma((count,))] * 8
        + [dma((groups,))] * 2
        + [dma((count,))] * 4,
        compiler_params=pltpu.CompilerParams(
            collective_id=0, has_side_effects=True, vmem_limit_bytes=56 * 2**20
        ),
        name="convolve_slices",
    )(jnp.asarray(coefs), *operands)
    half_out = jax.ShapeDtypeStruct((rows, chan_width), bf16)
    results = pl.pallas_call(
        finish_kernel,
        out_shape=(
            half_out,
            half_out,
            half_out,
            whole(share, chan_width),
            whole(3, chan_width),
            whole(1, chan_width),
            whole(feat, hidden_units),
            whole(hidden_units, hidden_units),
            whole(hidden_units, chan_width),
        ),
        in_specs=[vmem] * 5,
        out_specs=(vmem,) * 9,
        compiler_params=pltpu.CompilerParams(vmem_limit_bytes=60 * 2**20),
        name="finish_outputs",
    )(landed, small_landed, summed, query_branch, cotangent)
    return results[:5] + (results[5][0],) + results[6:]


def per_slice(*arrays):
    count = lax.axis_size("seq")
    rows, width = arrays[3].shape
    lanes = 2 * width // count
    units = arrays[7].shape[0]
    vocab = arrays[1].shape[0]
    tiled = lanes % 128 == 0 and rows % lanes == 0 and rows <= 8 * lanes
    even = count % 2 == 0 and 2 * units == lanes and units % (8 * count) == 0
    body = fused_device if tiled and even and vocab % (16 * count) == 0 else per_device
    return body(*arrays)


def solution(mesh):
    in_specs = (
        P("seq"),
        P(None, "chan"),
        P(None, "chan"),
        P("seq", "chan"),
        P("seq", "chan"),
        P("chan"),
        P(),
        P(),
        P(None, "chan"),
        P("chan"),
        P("seq", "chan"),
    )
    out_specs = (
        P("seq", "chan"),
        P("seq", "chan"),
        P("seq", "chan"),
        P("seq", "chan"),
        P(None, "chan"),
        P("chan"),
        P(),
        P(),
        P(None, "chan"),
    )
    return jax.shard_map(
        per_slice, mesh=mesh, in_specs=in_specs, out_specs=out_specs, check_vma=False
    )
```

```python
import functools
import math

import jax
import jax.numpy as jnp
import numpy as np
from jax import lax
from jax.experimental import pallas as pl
from jax.experimental.pallas import tpu as pltpu
from jax.sharding import PartitionSpec as P

BANDS = 16


highest = lax.Precision.HIGHEST
two_pi = 2.0 * math.pi


def from_behind(value, axis, steps):
    count = lax.axis_size(axis)
    leading, last = (max(0, -steps), min(count, count - steps))
    return lax.ppermute(value, axis, [(source, source + steps) for source in range(leading, last)])


def features(positions, length):
    frequency = 2 ** jnp.arange(BANDS, dtype=jnp.int32) + 1
    phases = positions[:, None] * frequency[None, :] % length
    angles = phases.astype(jnp.float32) * (two_pi / length)
    ramp_col = positions.astype(jnp.float32)[:, None] / length
    return jnp.concatenate([ramp_col, jnp.cos(angles), jnp.sin(angles)], axis=1)


def filter_forward(positions, length, weight_first, weight_second, weight_third, decay_rate):
    embedding = features(positions, length)
    pre_one = jnp.dot(
        embedding, weight_first, precision=highest, preferred_element_type=jnp.float32
    )
    act_one = jnp.sin(pre_one)
    pre_two = jnp.dot(act_one, weight_second, precision=highest, preferred_element_type=jnp.float32)
    act_two = jnp.sin(pre_two)
    shaped = jnp.dot(act_two, weight_third, precision=highest, preferred_element_type=jnp.float32)
    scaling = jnp.sqrt(jnp.expm1(-2.0 * decay_rate) / jnp.expm1(-2.0 * length * decay_rate))
    window = scaling[None, :] * jnp.exp(
        -decay_rate[None, :] * positions.astype(jnp.float32)[:, None]
    )
    return (shaped * window, (window, embedding, pre_one, act_one, pre_two, act_two))


def filter_head(grad_filter, saved_acts, weight_third):
    window, embedding, pre_one, act_one, pre_two, act_two = saved_acts
    grad_shaped = grad_filter * window
    grad_third = jnp.dot(
        act_two.T, grad_shaped, precision=highest, preferred_element_type=jnp.float32
    )
    grad_act_two = jnp.dot(
        grad_shaped, weight_third.T, precision=highest, preferred_element_type=jnp.float32
    )
    return (grad_third, grad_act_two)


def filter_tail(grad_act_two, saved_acts, weight_second):
    window, embedding, pre_one, act_one, pre_two, act_two = saved_acts
    grad_pre_two = grad_act_two * jnp.cos(pre_two)
    grad_second = jnp.dot(
        act_one.T, grad_pre_two, precision=highest, preferred_element_type=jnp.float32
    )
    grad_act_one = jnp.dot(
        grad_pre_two, weight_second.T, precision=highest, preferred_element_type=jnp.float32
    )
    grad_pre_one = grad_act_one * jnp.cos(pre_one)
    grad_first = jnp.dot(
        embedding.T, grad_pre_one, precision=highest, preferred_element_type=jnp.float32
    )
    return (grad_first, grad_second)


def rotation(first_index, second_index, modulus):
    phases = first_index * second_index % modulus
    angles = phases.astype(jnp.float32) * (two_pi / modulus)
    return (jnp.cos(angles), jnp.sin(angles))


def lane_forward(lane_rows, seq_count, points):
    width, length = lane_rows.shape
    depth_rows = length // seq_count
    blocks = lane_rows.reshape(width, seq_count, depth_rows)
    source_index = jnp.arange(seq_count, dtype=jnp.int32)
    lane_index = jnp.arange(2 * seq_count, dtype=jnp.int32)
    cosine_part, sine_part = rotation(lane_index[:, None], source_index[None, :], 2 * seq_count)
    small_table = jnp.concatenate([cosine_part, -sine_part], axis=0)
    product = jnp.einsum("kn,cnm->ckm", small_table, blocks, precision=highest)
    real_part = product[:, : 2 * seq_count]
    imag_part = product[:, 2 * seq_count :]
    cos_twist, sin_twist = rotation(
        lane_index[:, None], jnp.arange(depth_rows, dtype=jnp.int32)[None, :], points
    )
    turned = jnp.stack(
        [
            real_part * cos_twist + imag_part * sin_twist,
            imag_part * cos_twist - real_part * sin_twist,
        ]
    )
    grid_index = jnp.arange(depth_rows, dtype=jnp.int32)
    cos_block, sin_block = rotation(grid_index[:, None], grid_index[None, :], depth_rows)
    tables = jnp.concatenate([cos_block, sin_block], axis=1)
    both_parts = jnp.einsum("rckm,mj->rckj", turned, tables, precision=highest)
    return jnp.stack(
        [
            both_parts[0, :, :, :depth_rows] + both_parts[1, :, :, depth_rows:],
            both_parts[1, :, :, :depth_rows] - both_parts[0, :, :, depth_rows:],
        ]
    )


def lane_inverse(spectrum, seq_count, points):
    width = spectrum.shape[1]
    depth_rows = spectrum.shape[3]
    grid_index = jnp.arange(depth_rows, dtype=jnp.int32)
    cos_block, sin_block = rotation(grid_index[:, None], grid_index[None, :], depth_rows)
    tables = jnp.concatenate([cos_block, sin_block], axis=1)
    both_parts = jnp.einsum("rckm,mj->rckj", spectrum, tables, precision=highest)
    real_part = both_parts[0, :, :, :depth_rows] - both_parts[1, :, :, depth_rows:]
    imag_part = both_parts[1, :, :, :depth_rows] + both_parts[0, :, :, depth_rows:]
    lane_index = jnp.arange(2 * seq_count, dtype=jnp.int32)
    cos_twist, sin_twist = rotation(lane_index[:, None], grid_index[None, :], points)
    turned = jnp.stack(
        [
            real_part * cos_twist - imag_part * sin_twist,
            imag_part * cos_twist + real_part * sin_twist,
        ]
    )
    source_index = jnp.arange(seq_count, dtype=jnp.int32)
    cosine_part, sine_part = rotation(source_index[:, None], lane_index[None, :], 2 * seq_count)
    back_table = jnp.stack([cosine_part, -sine_part]) / points
    result_rows = jnp.einsum("rnk,rckm->cnm", back_table, turned, precision=highest)
    return result_rows.reshape(width, seq_count * depth_rows)


def pointwise(spectra):
    keyed_spec, filter_spec, grad_spec = spectra
    conv_spec = jnp.stack(
        [
            keyed_spec[0] * filter_spec[0] - keyed_spec[1] * filter_spec[1],
            keyed_spec[0] * filter_spec[1] + keyed_spec[1] * filter_spec[0],
        ]
    )
    back_spec = jnp.stack(
        [
            filter_spec[0] * grad_spec[0] + filter_spec[1] * grad_spec[1],
            filter_spec[0] * grad_spec[1] - filter_spec[1] * grad_spec[0],
        ]
    )
    shape_spec = jnp.stack(
        [
            keyed_spec[0] * grad_spec[0] + keyed_spec[1] * grad_spec[1],
            keyed_spec[0] * grad_spec[1] - keyed_spec[1] * grad_spec[0],
        ]
    )
    return (conv_spec, back_spec, shape_spec)


def per_device(
    tokens,
    embed_table,
    short_conv,
    query_branch,
    key_branch,
    decay_rate,
    weight_first,
    weight_second,
    weight_third,
    skip_gain,
    cotangent,
):
    seq_count = lax.axis_size("seq")
    seq_index = lax.axis_index("seq")
    row_count = query_branch.shape[0]
    chan_width = query_branch.shape[1]
    length = row_count * seq_count
    points = 2 * length
    inv_root = 1.0 / math.sqrt(length)
    vocab_size = embed_table.shape[0]
    earlier = from_behind(tokens[row_count - 2 :], "seq", 1)
    window_ids = jnp.concatenate([earlier, tokens])
    row_start = seq_index * row_count
    window_pos = row_start + jnp.arange(row_count + 2, dtype=jnp.int32) - 2
    present = window_pos >= 0
    vocab_ids = jnp.arange(vocab_size, dtype=jnp.int32)
    lookup = ((window_ids[:, None] == vocab_ids[None, :]) & present[:, None]).astype(jnp.bfloat16)
    embedded = jnp.dot(lookup, embed_table, preferred_element_type=jnp.float32)
    value_branch = (
        short_conv[0] * embedded[2:]
        + short_conv[1] * embedded[1:-1]
        + short_conv[2] * embedded[:-2]
    )
    key_rows = key_branch.astype(jnp.float32)
    keyed_value = key_rows * value_branch
    query_rows = query_branch.astype(jnp.float32)
    grad_out = cotangent.astype(jnp.float32)
    grad_z = grad_out * query_rows
    slice_width = chan_width // seq_count
    chan_start = seq_index * slice_width
    third_slice = lax.dynamic_slice_in_dim(weight_third, chan_start, slice_width, 1)
    rate_slice = lax.dynamic_slice_in_dim(decay_rate, chan_start, slice_width, 0)
    all_positions = jnp.arange(length, dtype=jnp.int32)
    filter_full, tail_acts = filter_forward(
        all_positions, length, weight_first, weight_second, third_slice, rate_slice
    )
    keyed_lanes, grad_lanes = (
        lax.all_to_all(keyed_value.T, "seq", split_axis=0, concat_axis=1, tiled=True),
        lax.all_to_all(grad_z.T, "seq", split_axis=0, concat_axis=1, tiled=True),
    )
    spectra = (
        lane_forward(keyed_lanes, seq_count, points),
        lane_forward(filter_full.T, seq_count, points),
        lane_forward(grad_lanes, seq_count, points),
    )
    conv_spec, back_spec, shape_spec = pointwise(spectra)
    conv_lanes = lane_inverse(conv_spec, seq_count, points)
    back_lanes = lane_inverse(back_spec, seq_count, points)
    filter_lanes = lane_inverse(shape_spec, seq_count, points)
    conv_rows, back_rows = (
        lax.all_to_all(conv_lanes, "seq", split_axis=1, concat_axis=0, tiled=True),
        lax.all_to_all(back_lanes, "seq", split_axis=1, concat_axis=0, tiled=True),
    )
    convolved = conv_rows.T
    back_keyed = back_rows.T
    third_small, act_two_part = filter_head(filter_lanes.T, tail_acts, third_slice)
    third_part = lax.dynamic_update_slice(
        jnp.zeros((third_small.shape[0], chan_width), jnp.float32),
        third_small,
        (jnp.zeros((), jnp.int32), chan_start),
    )
    inner_sum = convolved + skip_gain * keyed_value
    operator_out = (query_rows * inner_sum).astype(jnp.bfloat16)
    grad_query = (grad_out * inner_sum).astype(jnp.bfloat16)
    grad_keyed = back_keyed + skip_gain * grad_z
    grad_key = (grad_keyed * value_branch).astype(jnp.bfloat16)
    grad_value = grad_keyed * key_rows
    short_part = jnp.stack(
        [
            jnp.sum(grad_value * embedded[2 - offset : 2 - offset + row_count], axis=0)
            for offset in range(3)
        ]
    )
    skip_part = jnp.sum(grad_z * keyed_value, axis=0)
    ids_stacked = jnp.concatenate([window_ids[2:], window_ids[1:-1], window_ids[:-2]])
    live_stacked = jnp.concatenate([present[2:], present[1:-1], present[:-2]])
    weighted = jnp.concatenate([short_conv[offset] * grad_value for offset in range(3)], axis=0)
    vocab_rows = jnp.arange(vocab_size // seq_count * lax.axis_size("seq"), dtype=jnp.int32)
    matches = ((vocab_rows[:, None] == ids_stacked[None, :]) & live_stacked[None, :]).astype(
        jnp.float32
    )
    grad_embed = (
        lax.psum_scatter(
            jnp.dot(matches, weighted, precision=highest, preferred_element_type=jnp.float32),
            "seq",
            scatter_dimension=0,
            tiled=True,
        )
        * inv_root
    )
    grad_act_two = lax.psum(act_two_part, "chan")
    first_part, second_part = filter_tail(grad_act_two, tail_acts, weight_second)
    grad_short, grad_skip, grad_third, grad_first, grad_second = lax.psum(
        (short_part, skip_part, third_part, first_part, second_part), "seq"
    )
    return (
        operator_out,
        grad_query,
        grad_key,
        grad_embed,
        grad_short * inv_root,
        grad_skip * inv_root,
        grad_first * inv_root,
        grad_second * inv_root,
        grad_third * inv_root,
    )

MESH = pl.DeviceIdType.MESH
f32 = jnp.float32
bf16 = jnp.bfloat16


def split(value):
    high = value.astype(bf16)
    return high, (value - high.astype(f32)).astype(bf16)


def dot(left, right):
    return jnp.dot(left, right, preferred_element_type=f32)


def dot_full(left, right, contract=((1,), (0,))):
    return lax.dot_general(
        left, right, (contract, ((), ())), precision=highest, preferred_element_type=f32
    )


def low_lanes(shape):
    return lax.broadcasted_iota(jnp.int32, shape, len(shape) - 1) < shape[-1] // 2


def swap(value):
    return pltpu.roll(value, value.shape[-1] // 2, value.ndim - 1)


def greet(devices):
    barrier = pltpu.get_barrier_semaphore()
    for device in devices:
        pl.semaphore_signal(barrier, inc=1, device_id=device, device_id_type=MESH)
    pl.semaphore_wait(barrier, len(devices))


def pack_rows(number, query, key, cotangent, out):
    lanes = out.shape[-1]
    block = number // 2 * lanes
    key_part = key[:, block : block + lanes].astype(f32)
    grad_part = cotangent[:, block : block + lanes].astype(f32) * query[
        :, block : block + lanes
    ].astype(f32)
    low = low_lanes(key_part.shape)
    if number % 2 == 0:
        packed = jnp.where(low, key_part, swap(grad_part))
    else:
        packed = jnp.where(low, swap(key_part), grad_part)
    out[number] = packed


def one_less_exp(value):
    series = 1.0 - value / 9.0
    for order in range(8, 1, -1):
        series = 1.0 - value / order * series
    return jnp.where(value < 0.25, value * series, 1.0 - jnp.exp(-value))


def fused_kernel(
    count,
    groups,
    coefs,
    tokens,
    embed_table,
    short_conv,
    query,
    key,
    cotangent,
    decay_rate,
    first,
    second,
    weight_third,
    skip_gain,
    feats,
    twiddles,
    tables,
    landed,
    small_landed,
    summed,
    held_inputs,
    input_sems,
    table_high,
    table_low,
    staged,
    arrived,
    token_rows,
    token_landed,
    state,
    filters,
    windows,
    total,
    shape_total,
    value,
    embedded,
    gated,
    onehot,
    acts,
    filter_spec,
    shape_spec,
    pay,
    small,
    by_chan,
    held,
    by_seq,
    token_send,
    token_recv,
    out_send,
    out_recv,
    back_send,
    back_recv,
    small_send,
    small_recv,
    chan_send,
    chan_recv,
    scatter_send,
    scatter_recv,
    gather_send,
    gather_recv,
):
    me = lax.axis_index("seq")
    chan = lax.axis_index("chan")
    sources = (
        (key, query, cotangent, tokens)
        + (first, second, feats, embed_table, short_conv, decay_rate, weight_third)
        + (skip_gain, twiddles, tables)
    )
    loads = [
        pltpu.make_async_copy(source, target, input_sems.at[n])
        for n, (source, target) in enumerate(zip(sources, held_inputs))
    ]
    for load in loads:
        load.start()
    key, query, cotangent, tokens, first, second, feats = held_inputs[:7]
    embed_table, short_conv, decay_rate, weight_third = held_inputs[7:11]
    skip_gain, twiddles, tables = held_inputs[11:]
    rows = key.shape[0]
    lanes = staged.shape[2]
    vocab = embed_table.shape[0]
    units = second.shape[0]
    feat = first.shape[0]
    length = count * rows
    share = vocab // count
    peers = [lax.rem(me + step, count) for step in range(1, count)]
    sources = [lax.rem(me + count - step, count) for step in range(1, count)]
    across = [lax.rem(chan + step, groups) for step in range(1, groups)]

    def post(source, target, send, recv, device):
        copy = pltpu.make_async_remote_copy(
            src_ref=source,
            dst_ref=target,
            send_sem=send,
            recv_sem=recv,
            device_id=device,
            device_id_type=MESH,
        )
        copy.start()
        return copy

    for load in loads[:4]:
        load.wait()
    token_rows[...] = jnp.zeros_like(token_rows)
    token_rows[: tokens.shape[0]] = tokens[...].astype(f32)
    for number in range(count):
        pack_rows(number, query, key, cotangent, staged)
    greet([(peer, chan) for peer in peers] + [(me, group) for group in across])
    token_copies = [
        post(token_rows, token_landed.at[me], token_send.at[n], token_recv.at[n], (peer, chan))
        for n, peer in enumerate(peers)
    ]
    out_copies = [
        post(staged.at[peer], arrived.at[me], out_send.at[n], out_recv.at[n], (peer, chan))
        for n, peer in enumerate(peers)
    ]
    arrived[me] = staged[me]
    token_landed[me] = token_rows[...]

    for load in loads[4:]:
        load.wait()
    table_high[...], table_low[...] = split(tables[...])

    columns = pl.ds(pl.multiple_of(me // 2 * lanes, lanes), lanes)
    parity = lax.rem(me, 2)

    def mine(array):
        lane = lax.broadcasted_iota(jnp.int32, array.shape, 1)
        return jnp.where(lane // (lanes // 2) == parity, array, swap(array))

    third = mine(weight_third[:, columns])
    table = mine(embed_table[:, columns].astype(f32)).astype(bf16)
    rate = mine(jnp.broadcast_to(decay_rate[:, columns], (8, lanes)))[:1]
    skip = mine(jnp.broadcast_to(skip_gain[:, columns], (8, lanes)))[:1]
    all_taps = [mine(jnp.broadcast_to(short_conv[j : j + 1, columns], (8, lanes))) for j in range(3)]
    taps = [tap[:1] for tap in all_taps]
    scale = jnp.sqrt(one_less_exp(2.0 * rate) / one_less_exp(2.0 * length * rate))
    low = low_lanes((rows, lanes))
    sign = jnp.where(low, 1.0, -1.0).astype(f32)

    pre_one = dot_full(first[...], feats[:feat], ((0,), (0,)))
    act_one = jnp.sin(pre_one)
    acts[0] = act_one
    acts[1] = jnp.cos(pre_one)
    pre_two = dot_full(second[...], act_one, ((0,), (0,)))
    acts[2] = jnp.sin(pre_two)
    acts[3] = jnp.cos(pre_two)
    row_ids = lax.broadcasted_iota(jnp.int32, (rows, lanes), 0).astype(f32)
    for block in range(count):
        act_rows = acts[2, :, block * rows : (block + 1) * rows].T
        window = scale * jnp.exp(-rate * (row_ids + float(block * rows)))
        windows[block] = window
        filters[block] = dot_full(act_rows, third) * window

    def spread(both):
        high, rest = split(both)
        product = (
            dot(table_high[...], high) + dot(table_high[...], rest) + dot(table_low[...], high)
        )
        return product[:rows], product[rows:]

    def turn_forward(real, imag, lane):
        cos_t = twiddles[lane, 0]
        sin_t = twiddles[lane, 1]
        by_cos, by_sin = spread(
            jnp.concatenate([real * cos_t + imag * sin_t, imag * cos_t - real * sin_t], axis=1)
        )
        return (
            by_cos[:, :lanes] + by_sin[:, lanes:],
            by_cos[:, lanes:] - by_sin[:, :lanes],
        )

    def forward(ref, lane):
        cos_sums, sin_sums = [], []
        for start in range(2):
            cos_sum = jnp.zeros((rows, lanes), f32)
            sin_sum = jnp.zeros((rows, lanes), f32)
            for n in range(start, count, 2):
                piece = ref[n]
                cos_sum = cos_sum + coefs[lane, n] * piece
                sin_sum = sin_sum + coefs[lane, count + n] * piece
            cos_sums.append(cos_sum)
            sin_sums.append(sin_sum)
        return (
            turn_forward(cos_sums[0] + cos_sums[1], -(sin_sums[0] + sin_sums[1]), lane),
            turn_forward(cos_sums[0] - cos_sums[1], sin_sums[0] - sin_sums[1], count - lane),
        )

    def add_back(ref, lane, near, far):
        (near_cos, near_sin), (far_cos, far_sin) = near, far
        by_parity = (
            (near_cos + far_cos, near_sin - far_sin),
            (near_cos - far_cos, near_sin + far_sin),
        )
        for n in range(count):
            cos_part, sin_part = by_parity[n % 2]
            ref[n] += (
                coefs[lane, 2 * count + n] * cos_part - coefs[lane, 3 * count + n] * sin_part
            )

    def transform_filter(lane, carry):
        for place, (real, imag) in zip((lane, count - lane), forward(filters, lane)):
            filter_spec[place, 0] = real
            filter_spec[place, 1] = imag * sign
        return carry

    lax.fori_loop(0, count // 2 + 1, transform_filter, 0)

    for copy in token_copies:
        copy.wait()
    embedded[:8] = jnp.zeros((8, lanes), f32)
    vocab_ids = lax.broadcasted_iota(jnp.int32, (vocab, lanes), 0).astype(f32)
    for block in range(count):
        for piece in range(rows // lanes):
            ids = token_landed[block, piece : piece + 1]
            matches = jnp.where(vocab_ids == ids, 1.0, 0.0)
            start = block * rows + piece * lanes
            onehot[:, start : start + lanes] = matches.astype(bf16)
            embedded[8 + start : 8 + start + lanes] = dot(matches.T.astype(bf16), table)
    for block in range(count):
        start = 8 + block * rows
        value[block] = (
            taps[0] * embedded[start : start + rows]
            + taps[1] * embedded[start - 1 : start - 1 + rows]
            + taps[2] * embedded[start - 2 : start - 2 + rows]
        )
    total[...] = jnp.zeros_like(total)
    shape_total[...] = jnp.zeros_like(shape_total)

    def gate(block):
        packed = arrived[block]
        state[block] = jnp.where(low, packed * value[block], packed)

    gate(me)
    for copy, source in zip(out_copies, sources):
        copy.wait()
        gate(source)

    def multiply(place, xr, xi):
        fr = filter_spec[place, 0]
        fi = filter_spec[place, 1]
        by_cos, by_sin = spread(jnp.concatenate([xr * fr - xi * fi, xr * fi + xi * fr], axis=1))
        zr = by_cos[:, :lanes] - by_sin[:, lanes:]
        zi = by_cos[:, lanes:] + by_sin[:, :lanes]
        cos_t = twiddles[place, 0]
        sin_t = twiddles[place, 1]
        gr, gi = swap(xr), swap(xi)
        shape_spec[place] = jnp.where(low, xr * gr + xi * gi, swap(xr * gi - xi * gr))
        return zr * cos_t - zi * sin_t, zr * sin_t + zi * cos_t

    def convolve(lane, carry):
        near, far = forward(state, lane)
        add_back(total, lane, multiply(lane, *near), multiply(count - lane, *far))
        return carry

    lax.fori_loop(0, count // 2 + 1, convolve, 0)

    def finish(block):
        summed_rows = total[block] + skip * state[block]
        total[block] = summed_rows
        return jnp.where(low, summed_rows, summed_rows * value[block])

    middle = rows // 2

    def post_back(n, part):
        places = pl.ds(part * middle, middle)
        return post(
            pay.at[peers[n], places],
            landed.at[me, places],
            back_send.at[part, n],
            back_recv.at[part, n],
            (peers[n], chan),
        )

    back_copies = []
    for n, peer in enumerate(peers):
        pay[peer] = finish(peer)
        back_copies.append(post_back(n, 0))
    landed[me] = finish(me)

    def correlate_one(place):
        cos_t = twiddles[place, 0]
        sin_t = twiddles[place, 1]
        by_cos, by_sin = spread(shape_spec[place])
        both = by_cos - sign * swap(by_sin)
        return both * jnp.where(low, cos_t, -sin_t), both * jnp.where(low, sin_t, cos_t)

    def correlate(lane, carry):
        add_back(shape_total, lane, correlate_one(lane), correlate_one(count - lane))
        return carry

    lax.fori_loop(0, count // 2 + 1, correlate, 0)
    inv_root = 1.0 / math.sqrt(length)
    third_sum = jnp.zeros((units, lanes), f32)
    third_low = jnp.where(low_lanes(third.shape), third, 0.0)
    for block in range(count):
        grad_rows = shape_total[block]
        grad_rows = (grad_rows + swap(grad_rows)) * windows[block]
        places = slice(block * rows, (block + 1) * rows)
        third_sum += dot_full(acts[2, :, places], grad_rows)
        acts[3, :, places] = dot_full(third_low, grad_rows, ((1,), (1,))) * acts[3, :, places]
    grad_pre_two = acts[3]
    grad_pre_one = dot_full(second[...], grad_pre_two) * acts[1]
    grad_both = jnp.concatenate([grad_pre_two, grad_pre_one], axis=0)
    from_act = dot_full(acts[0], grad_both, ((1,), (1,)))
    from_feats = dot_full(feats[...], grad_both, ((1,), (1,)))
    hidden = jnp.where(low_lanes(from_act.shape), from_act, from_feats) * inv_root
    strip = units // count
    for n in range(count):
        by_chan[chan, n] = hidden[n * strip : (n + 1) * strip]
    chan_copies = [
        post(by_chan.at[chan], by_chan.at[chan], chan_send.at[n], chan_recv.at[n], (me, group))
        for n, group in enumerate(across)
    ]

    for copy in chan_copies:
        copy.wait()
    for n in range(count):
        strip_sum = by_chan[0, n]
        for group in range(1, groups):
            strip_sum = strip_sum + by_chan[group, n]
        held[n] = strip_sum
    scatter_copies = [
        post(held.at[peer], by_seq.at[me], scatter_send.at[n], scatter_recv.at[n], (peer, chan))
        for n, peer in enumerate(peers)
    ]
    by_seq[me] = held[me]
    back_copies += [post_back(n, 1) for n in range(count - 1)]

    gated[length:] = jnp.zeros((8, lanes), f32)
    short_sums = [jnp.zeros((1, lanes), f32) for _ in range(3)]
    skip_sum = jnp.zeros((1, lanes), f32)
    for block in range(count):
        start = block * rows
        grad_value = total[block] * swap(arrived[block])
        gated[start : start + rows] = grad_value
        for j in range(3):
            short_sums[j] += jnp.sum(
                grad_value * embedded[8 + start - j : 8 + start - j + rows], axis=0, keepdims=True
            )
        skip_sum += jnp.sum(state[block] * swap(state[block]), axis=0, keepdims=True)
    embed_sum = jnp.zeros((vocab, lanes), f32)
    for block in range(count):
        start = block * rows
        high, rest = split(
            taps[0] * gated[start : start + rows]
            + taps[1] * gated[start + 1 : start + 1 + rows]
            + taps[2] * gated[start + 2 : start + 2 + rows]
        )
        matches = onehot[:, start : start + rows]
        embed_sum += dot(matches, high) + dot(matches, rest)
    half = units // 2
    fold = jnp.where(low_lanes((half, lanes)), third_sum[:half], third_sum[half:])
    sums = jnp.concatenate([fold, *short_sums, skip_sum, jnp.zeros((4, lanes), f32)], axis=0)
    for block in range(count):
        top = embed_sum[block * share : block * share + share // 2]
        bottom = embed_sum[block * share + share // 2 : (block + 1) * share]
        folded = jnp.where(low_lanes(top.shape), swap(top), bottom)
        small[block] = jnp.concatenate([folded, sums], axis=0) * inv_root
    small_copies = [
        post(small.at[peer], small_landed.at[me], small_send.at[n], small_recv.at[n], (peer, chan))
        for n, peer in enumerate(peers)
    ]
    small_landed[me] = small[me]

    for copy in scatter_copies:
        copy.wait()
    strip_sum = by_seq[0]
    for n in range(1, count):
        strip_sum = strip_sum + by_seq[n]
    summed[me] = strip_sum
    gather_copies = [
        post(summed.at[me], summed.at[me], gather_send.at[n], gather_recv.at[n], (peer, chan))
        for n, peer in enumerate(peers)
    ]
    for copy in back_copies + small_copies + gather_copies:
        copy.wait()


def finish_kernel(
    landed,
    small_landed,
    summed,
    query,
    cotangent,
    out,
    grad_query,
    grad_key,
    grad_embed,
    grad_short,
    grad_skip,
    grad_first,
    grad_second,
    grad_third,
):
    count, rows, lanes = landed.shape
    low = low_lanes((rows, lanes))
    share = grad_embed.shape[0]
    part = share // 2
    half = grad_third.shape[0] // 2
    for block in range(count // 2):
        columns = slice(block * lanes, (block + 1) * lanes)
        even, odd = landed[2 * block], landed[2 * block + 1]
        inner = jnp.where(low, even, swap(odd))
        out[:, columns] = (query[:, columns].astype(f32) * inner).astype(bf16)
        grad_query[:, columns] = (cotangent[:, columns].astype(f32) * inner).astype(bf16)
        grad_key[:, columns] = jnp.where(low, swap(even), odd).astype(bf16)
        even, odd = small_landed[2 * block], small_landed[2 * block + 1]
        left = low_lanes(even.shape)
        first_rows = jnp.where(left, even, swap(odd))
        last_rows = jnp.where(left, swap(even), odd)
        grad_embed[:part, columns] = first_rows[:part]
        grad_embed[part:, columns] = last_rows[:part]
        grad_third[:half, columns] = first_rows[part : part + half]
        grad_third[half:, columns] = last_rows[part : part + half]
        top = part + half
        grad_short[:, columns] = last_rows[top : top + 3]
        grad_skip[:, columns] = last_rows[top + 3 : top + 4]
    both = jnp.concatenate([summed[n] for n in range(count)], axis=0)
    units = grad_second.shape[0]
    grad_second[...] = both[:, :units]
    grad_first[...] = swap(both)[: grad_first.shape[0], :units]


def feature_table(length):
    positions = np.arange(length, dtype=np.int64)
    frequency = 2 ** np.arange(BANDS, dtype=np.int64) + 1
    phases = positions[:, None] * frequency[None, :] % length
    angles = phases.astype(np.float32) * np.float32(two_pi / length)
    ramp = positions.astype(np.float32)[:, None] / np.float32(length)
    return np.concatenate([ramp, np.cos(angles), np.sin(angles)], axis=1).T.astype(np.float32)


def fused_device(
    tokens,
    embed_table,
    short_conv,
    query_branch,
    key_branch,
    decay_rate,
    weight_first,
    weight_second,
    weight_third,
    skip_gain,
    cotangent,
):
    count = lax.axis_size("seq")
    groups = lax.axis_size("chan")
    seq_index = lax.axis_index("seq")
    rows, chan_width = query_branch.shape
    length = rows * count
    points = 2 * length
    vocab = embed_table.shape[0]
    hidden_units = weight_second.shape[0]
    feat = weight_first.shape[0]
    slice_width = chan_width // count
    lanes = 2 * slice_width
    share = vocab // count
    strip = hidden_units // count
    small_rows = share // 2 + hidden_units // 2 + 8
    vmem = pl.BlockSpec(memory_space=pltpu.VMEM)
    smem = pl.BlockSpec(memory_space=pltpu.SMEM)
    dma = pltpu.SemaphoreType.DMA

    depth = np.arange(rows)
    turns = np.arange(count + 1)
    angle = two_pi * (depth[:, None] * depth[None, :] % rows) / rows
    tables = np.concatenate([np.cos(angle), np.sin(angle)], axis=0).astype(np.float32)
    twist = two_pi * (turns[:, None] * depth[None, :]) / points
    twiddles = np.stack([np.cos(twist), np.sin(twist)], axis=1).astype(np.float32)
    twiddles = np.broadcast_to(twiddles[..., None], (count + 1, 2, rows, lanes)).copy()
    small_angle = two_pi * (turns[:, None] * np.arange(count)[None, :] % (2 * count)) / (2 * count)
    weight = np.where(turns % (count // 2) == 0, 1.0, 2.0)[:, None] / points
    coefs = np.concatenate(
        [
            np.cos(small_angle),
            np.sin(small_angle),
            weight * np.cos(small_angle),
            weight * np.sin(small_angle),
        ],
        axis=1,
    ).astype(np.float32)
    feats = np.pad(feature_table(length), ((0, hidden_units - feat), (0, 0)))

    def whole(*shape):
        return jax.ShapeDtypeStruct(shape, f32)

    def buffer(*shape):
        return pltpu.VMEM(shape, f32)

    block_shape = (count, rows, lanes)
    operands = (
        tokens.reshape(rows // lanes, lanes),
        embed_table,
        short_conv,
        query_branch,
        key_branch,
        cotangent,
        decay_rate[None],
        weight_first,
        weight_second,
        weight_third,
        skip_gain[None],
        jnp.asarray(feats),
        jnp.asarray(twiddles),
        jnp.asarray(tables),
    )
    load_order = (4, 3, 5, 0, 7, 8, 11, 1, 2, 6, 9, 10, 12, 13)
    landed, small_landed, summed = pl.pallas_call(
        functools.partial(fused_kernel, count, groups),
        out_shape=(
            whole(*block_shape),
            whole(count, small_rows, lanes),
            whole(count, strip, lanes),
        ),
        in_specs=[smem] + [pl.BlockSpec(memory_space=pltpu.HBM)] * 14,
        out_specs=(vmem,) * 3,
        scratch_shapes=[
            [pltpu.VMEM(operands[n].shape, operands[n].dtype) for n in load_order],
            dma((len(load_order),)),
            pltpu.VMEM(tables.shape, bf16),
            pltpu.VMEM(tables.shape, bf16),
            buffer(*block_shape),
            buffer(*block_shape),
            buffer(8, lanes),
            buffer(count, 8, lanes),
            buffer(*block_shape),
            buffer(*block_shape),
            buffer(*block_shape),
            buffer(*block_shape),
            buffer(*block_shape),
            buffer(*block_shape),
            buffer(length + 8, lanes),
            buffer(length + 8, lanes),
            pltpu.VMEM((vocab, length), bf16),
            buffer(4, hidden_units, length),
            buffer(count + 1, 2, rows, lanes),
            buffer(count + 1, rows, lanes),
            buffer(*block_shape),
            buffer(count, small_rows, lanes),
            buffer(groups, count, strip, lanes),
            buffer(count, strip, lanes),
            buffer(count, strip, lanes),
        ]
        + [dma((count,))] * 4
        + [dma((2, count))] * 2
        + [dma((count,))] * 2
        + [dma((groups,))] * 2
        + [dma((count,))] * 4,
        compiler_params=pltpu.CompilerParams(
            collective_id=0, has_side_effects=True, vmem_limit_bytes=56 * 2**20
        ),
        name="convolve_slices",
    )(jnp.asarray(coefs), *operands)
    half_out = jax.ShapeDtypeStruct((rows, chan_width), bf16)
    results = pl.pallas_call(
        finish_kernel,
        out_shape=(
            half_out,
            half_out,
            half_out,
            whole(share, chan_width),
            whole(3, chan_width),
            whole(1, chan_width),
            whole(feat, hidden_units),
            whole(hidden_units, hidden_units),
            whole(hidden_units, chan_width),
        ),
        in_specs=[vmem] * 5,
        out_specs=(vmem,) * 9,
        compiler_params=pltpu.CompilerParams(vmem_limit_bytes=60 * 2**20),
        name="finish_outputs",
    )(landed, small_landed, summed, query_branch, cotangent)
    return results[:5] + (results[5][0],) + results[6:]


def per_slice(*arrays):
    count = lax.axis_size("seq")
    rows, width = arrays[3].shape
    lanes = 2 * width // count
    units = arrays[7].shape[0]
    vocab = arrays[1].shape[0]
    tiled = lanes % 128 == 0 and rows % lanes == 0 and rows <= 8 * lanes
    even = count % 2 == 0 and 2 * units == lanes and units % (8 * count) == 0
    body = fused_device if tiled and even and vocab % (16 * count) == 0 else per_device
    return body(*arrays)


def solution(mesh):
    in_specs = (
        P("seq"),
        P(None, "chan"),
        P(None, "chan"),
        P("seq", "chan"),
        P("seq", "chan"),
        P("chan"),
        P(),
        P(),
        P(None, "chan"),
        P("chan"),
        P("seq", "chan"),
    )
    out_specs = (
        P("seq", "chan"),
        P("seq", "chan"),
        P("seq", "chan"),
        P("seq", "chan"),
        P(None, "chan"),
        P("chan"),
        P(),
        P(),
        P(None, "chan"),
    )
    return jax.shard_map(
        per_slice, mesh=mesh, in_specs=in_specs, out_specs=out_specs, check_vma=False
    )
```

```python
import functools
import math

import jax
import jax.numpy as jnp
import numpy as np
from jax import lax
from jax.experimental import pallas as pl
from jax.experimental.pallas import tpu as pltpu
from jax.sharding import PartitionSpec as P

BANDS = 16


highest = lax.Precision.HIGHEST
two_pi = 2.0 * math.pi


def from_behind(value, axis, steps):
    count = lax.axis_size(axis)
    leading, last = (max(0, -steps), min(count, count - steps))
    return lax.ppermute(value, axis, [(source, source + steps) for source in range(leading, last)])


def features(positions, length):
    frequency = 2 ** jnp.arange(BANDS, dtype=jnp.int32) + 1
    phases = positions[:, None] * frequency[None, :] % length
    angles = phases.astype(jnp.float32) * (two_pi / length)
    ramp_col = positions.astype(jnp.float32)[:, None] / length
    return jnp.concatenate([ramp_col, jnp.cos(angles), jnp.sin(angles)], axis=1)


def filter_forward(positions, length, weight_first, weight_second, weight_third, decay_rate):
    embedding = features(positions, length)
    pre_one = jnp.dot(
        embedding, weight_first, precision=highest, preferred_element_type=jnp.float32
    )
    act_one = jnp.sin(pre_one)
    pre_two = jnp.dot(act_one, weight_second, precision=highest, preferred_element_type=jnp.float32)
    act_two = jnp.sin(pre_two)
    shaped = jnp.dot(act_two, weight_third, precision=highest, preferred_element_type=jnp.float32)
    scaling = jnp.sqrt(jnp.expm1(-2.0 * decay_rate) / jnp.expm1(-2.0 * length * decay_rate))
    window = scaling[None, :] * jnp.exp(
        -decay_rate[None, :] * positions.astype(jnp.float32)[:, None]
    )
    return (shaped * window, (window, embedding, pre_one, act_one, pre_two, act_two))


def filter_head(grad_filter, saved_acts, weight_third):
    window, embedding, pre_one, act_one, pre_two, act_two = saved_acts
    grad_shaped = grad_filter * window
    grad_third = jnp.dot(
        act_two.T, grad_shaped, precision=highest, preferred_element_type=jnp.float32
    )
    grad_act_two = jnp.dot(
        grad_shaped, weight_third.T, precision=highest, preferred_element_type=jnp.float32
    )
    return (grad_third, grad_act_two)


def filter_tail(grad_act_two, saved_acts, weight_second):
    window, embedding, pre_one, act_one, pre_two, act_two = saved_acts
    grad_pre_two = grad_act_two * jnp.cos(pre_two)
    grad_second = jnp.dot(
        act_one.T, grad_pre_two, precision=highest, preferred_element_type=jnp.float32
    )
    grad_act_one = jnp.dot(
        grad_pre_two, weight_second.T, precision=highest, preferred_element_type=jnp.float32
    )
    grad_pre_one = grad_act_one * jnp.cos(pre_one)
    grad_first = jnp.dot(
        embedding.T, grad_pre_one, precision=highest, preferred_element_type=jnp.float32
    )
    return (grad_first, grad_second)


def rotation(first_index, second_index, modulus):
    phases = first_index * second_index % modulus
    angles = phases.astype(jnp.float32) * (two_pi / modulus)
    return (jnp.cos(angles), jnp.sin(angles))


def lane_forward(lane_rows, seq_count, points):
    width, length = lane_rows.shape
    depth_rows = length // seq_count
    blocks = lane_rows.reshape(width, seq_count, depth_rows)
    source_index = jnp.arange(seq_count, dtype=jnp.int32)
    lane_index = jnp.arange(2 * seq_count, dtype=jnp.int32)
    cosine_part, sine_part = rotation(lane_index[:, None], source_index[None, :], 2 * seq_count)
    small_table = jnp.concatenate([cosine_part, -sine_part], axis=0)
    product = jnp.einsum("kn,cnm->ckm", small_table, blocks, precision=highest)
    real_part = product[:, : 2 * seq_count]
    imag_part = product[:, 2 * seq_count :]
    cos_twist, sin_twist = rotation(
        lane_index[:, None], jnp.arange(depth_rows, dtype=jnp.int32)[None, :], points
    )
    turned = jnp.stack(
        [
            real_part * cos_twist + imag_part * sin_twist,
            imag_part * cos_twist - real_part * sin_twist,
        ]
    )
    grid_index = jnp.arange(depth_rows, dtype=jnp.int32)
    cos_block, sin_block = rotation(grid_index[:, None], grid_index[None, :], depth_rows)
    tables = jnp.concatenate([cos_block, sin_block], axis=1)
    both_parts = jnp.einsum("rckm,mj->rckj", turned, tables, precision=highest)
    return jnp.stack(
        [
            both_parts[0, :, :, :depth_rows] + both_parts[1, :, :, depth_rows:],
            both_parts[1, :, :, :depth_rows] - both_parts[0, :, :, depth_rows:],
        ]
    )


def lane_inverse(spectrum, seq_count, points):
    width = spectrum.shape[1]
    depth_rows = spectrum.shape[3]
    grid_index = jnp.arange(depth_rows, dtype=jnp.int32)
    cos_block, sin_block = rotation(grid_index[:, None], grid_index[None, :], depth_rows)
    tables = jnp.concatenate([cos_block, sin_block], axis=1)
    both_parts = jnp.einsum("rckm,mj->rckj", spectrum, tables, precision=highest)
    real_part = both_parts[0, :, :, :depth_rows] - both_parts[1, :, :, depth_rows:]
    imag_part = both_parts[1, :, :, :depth_rows] + both_parts[0, :, :, depth_rows:]
    lane_index = jnp.arange(2 * seq_count, dtype=jnp.int32)
    cos_twist, sin_twist = rotation(lane_index[:, None], grid_index[None, :], points)
    turned = jnp.stack(
        [
            real_part * cos_twist - imag_part * sin_twist,
            imag_part * cos_twist + real_part * sin_twist,
        ]
    )
    source_index = jnp.arange(seq_count, dtype=jnp.int32)
    cosine_part, sine_part = rotation(source_index[:, None], lane_index[None, :], 2 * seq_count)
    back_table = jnp.stack([cosine_part, -sine_part]) / points
    result_rows = jnp.einsum("rnk,rckm->cnm", back_table, turned, precision=highest)
    return result_rows.reshape(width, seq_count * depth_rows)


def pointwise(spectra):
    keyed_spec, filter_spec, grad_spec = spectra
    conv_spec = jnp.stack(
        [
            keyed_spec[0] * filter_spec[0] - keyed_spec[1] * filter_spec[1],
            keyed_spec[0] * filter_spec[1] + keyed_spec[1] * filter_spec[0],
        ]
    )
    back_spec = jnp.stack(
        [
            filter_spec[0] * grad_spec[0] + filter_spec[1] * grad_spec[1],
            filter_spec[0] * grad_spec[1] - filter_spec[1] * grad_spec[0],
        ]
    )
    shape_spec = jnp.stack(
        [
            keyed_spec[0] * grad_spec[0] + keyed_spec[1] * grad_spec[1],
            keyed_spec[0] * grad_spec[1] - keyed_spec[1] * grad_spec[0],
        ]
    )
    return (conv_spec, back_spec, shape_spec)


def per_device(
    tokens,
    embed_table,
    short_conv,
    query_branch,
    key_branch,
    decay_rate,
    weight_first,
    weight_second,
    weight_third,
    skip_gain,
    cotangent,
):
    seq_count = lax.axis_size("seq")
    seq_index = lax.axis_index("seq")
    row_count = query_branch.shape[0]
    chan_width = query_branch.shape[1]
    length = row_count * seq_count
    points = 2 * length
    inv_root = 1.0 / math.sqrt(length)
    vocab_size = embed_table.shape[0]
    earlier = from_behind(tokens[row_count - 2 :], "seq", 1)
    window_ids = jnp.concatenate([earlier, tokens])
    row_start = seq_index * row_count
    window_pos = row_start + jnp.arange(row_count + 2, dtype=jnp.int32) - 2
    present = window_pos >= 0
    vocab_ids = jnp.arange(vocab_size, dtype=jnp.int32)
    lookup = ((window_ids[:, None] == vocab_ids[None, :]) & present[:, None]).astype(jnp.bfloat16)
    embedded = jnp.dot(lookup, embed_table, preferred_element_type=jnp.float32)
    value_branch = (
        short_conv[0] * embedded[2:]
        + short_conv[1] * embedded[1:-1]
        + short_conv[2] * embedded[:-2]
    )
    key_rows = key_branch.astype(jnp.float32)
    keyed_value = key_rows * value_branch
    query_rows = query_branch.astype(jnp.float32)
    grad_out = cotangent.astype(jnp.float32)
    grad_z = grad_out * query_rows
    slice_width = chan_width // seq_count
    chan_start = seq_index * slice_width
    third_slice = lax.dynamic_slice_in_dim(weight_third, chan_start, slice_width, 1)
    rate_slice = lax.dynamic_slice_in_dim(decay_rate, chan_start, slice_width, 0)
    all_positions = jnp.arange(length, dtype=jnp.int32)
    filter_full, tail_acts = filter_forward(
        all_positions, length, weight_first, weight_second, third_slice, rate_slice
    )
    keyed_lanes, grad_lanes = (
        lax.all_to_all(keyed_value.T, "seq", split_axis=0, concat_axis=1, tiled=True),
        lax.all_to_all(grad_z.T, "seq", split_axis=0, concat_axis=1, tiled=True),
    )
    spectra = (
        lane_forward(keyed_lanes, seq_count, points),
        lane_forward(filter_full.T, seq_count, points),
        lane_forward(grad_lanes, seq_count, points),
    )
    conv_spec, back_spec, shape_spec = pointwise(spectra)
    conv_lanes = lane_inverse(conv_spec, seq_count, points)
    back_lanes = lane_inverse(back_spec, seq_count, points)
    filter_lanes = lane_inverse(shape_spec, seq_count, points)
    conv_rows, back_rows = (
        lax.all_to_all(conv_lanes, "seq", split_axis=1, concat_axis=0, tiled=True),
        lax.all_to_all(back_lanes, "seq", split_axis=1, concat_axis=0, tiled=True),
    )
    convolved = conv_rows.T
    back_keyed = back_rows.T
    third_small, act_two_part = filter_head(filter_lanes.T, tail_acts, third_slice)
    third_part = lax.dynamic_update_slice(
        jnp.zeros((third_small.shape[0], chan_width), jnp.float32),
        third_small,
        (jnp.zeros((), jnp.int32), chan_start),
    )
    inner_sum = convolved + skip_gain * keyed_value
    operator_out = (query_rows * inner_sum).astype(jnp.bfloat16)
    grad_query = (grad_out * inner_sum).astype(jnp.bfloat16)
    grad_keyed = back_keyed + skip_gain * grad_z
    grad_key = (grad_keyed * value_branch).astype(jnp.bfloat16)
    grad_value = grad_keyed * key_rows
    short_part = jnp.stack(
        [
            jnp.sum(grad_value * embedded[2 - offset : 2 - offset + row_count], axis=0)
            for offset in range(3)
        ]
    )
    skip_part = jnp.sum(grad_z * keyed_value, axis=0)
    ids_stacked = jnp.concatenate([window_ids[2:], window_ids[1:-1], window_ids[:-2]])
    live_stacked = jnp.concatenate([present[2:], present[1:-1], present[:-2]])
    weighted = jnp.concatenate([short_conv[offset] * grad_value for offset in range(3)], axis=0)
    vocab_rows = jnp.arange(vocab_size // seq_count * lax.axis_size("seq"), dtype=jnp.int32)
    matches = ((vocab_rows[:, None] == ids_stacked[None, :]) & live_stacked[None, :]).astype(
        jnp.float32
    )
    grad_embed = (
        lax.psum_scatter(
            jnp.dot(matches, weighted, precision=highest, preferred_element_type=jnp.float32),
            "seq",
            scatter_dimension=0,
            tiled=True,
        )
        * inv_root
    )
    grad_act_two = lax.psum(act_two_part, "chan")
    first_part, second_part = filter_tail(grad_act_two, tail_acts, weight_second)
    grad_short, grad_skip, grad_third, grad_first, grad_second = lax.psum(
        (short_part, skip_part, third_part, first_part, second_part), "seq"
    )
    return (
        operator_out,
        grad_query,
        grad_key,
        grad_embed,
        grad_short * inv_root,
        grad_skip * inv_root,
        grad_first * inv_root,
        grad_second * inv_root,
        grad_third * inv_root,
    )

MESH = pl.DeviceIdType.MESH
f32 = jnp.float32
bf16 = jnp.bfloat16


def split(value):
    high = value.astype(bf16)
    return high, (value - high.astype(f32)).astype(bf16)


def dot(left, right):
    return jnp.dot(left, right, preferred_element_type=f32)


def dot_full(left, right, contract=((1,), (0,))):
    return lax.dot_general(
        left, right, (contract, ((), ())), precision=highest, preferred_element_type=f32
    )


def low_lanes(shape):
    return lax.broadcasted_iota(jnp.int32, shape, len(shape) - 1) < shape[-1] // 2


def swap(value):
    return pltpu.roll(value, value.shape[-1] // 2, value.ndim - 1)


def greet(devices):
    barrier = pltpu.get_barrier_semaphore()
    for device in devices:
        pl.semaphore_signal(barrier, inc=1, device_id=device, device_id_type=MESH)


def pack_rows(number, query, key, cotangent, out):
    lanes = out.shape[-1]
    block = number // 2 * lanes
    key_part = key[:, block : block + lanes].astype(f32)
    grad_part = cotangent[:, block : block + lanes].astype(f32) * query[
        :, block : block + lanes
    ].astype(f32)
    low = low_lanes(key_part.shape)
    if number % 2 == 0:
        packed = jnp.where(low, key_part, swap(grad_part))
    else:
        packed = jnp.where(low, swap(key_part), grad_part)
    out[number] = packed


def one_less_exp(value):
    series = 1.0 - value / 9.0
    for order in range(8, 1, -1):
        series = 1.0 - value / order * series
    return jnp.where(value < 0.25, value * series, 1.0 - jnp.exp(-value))


def fused_kernel(
    count,
    groups,
    coefs,
    tokens,
    embed_table,
    short_conv,
    query,
    key,
    cotangent,
    decay_rate,
    first,
    second,
    weight_third,
    skip_gain,
    feats,
    twiddles,
    tables,
    landed,
    small_landed,
    summed,
    held_inputs,
    input_sems,
    table_high,
    table_low,
    staged,
    arrived,
    token_rows,
    token_landed,
    state,
    filters,
    windows,
    total,
    shape_total,
    value,
    embedded,
    gated,
    onehot,
    acts,
    filter_spec,
    shape_spec,
    pay,
    small,
    by_chan,
    held,
    by_seq,
    token_send,
    token_recv,
    out_send,
    out_recv,
    back_send,
    back_recv,
    small_send,
    small_recv,
    chan_send,
    chan_recv,
    scatter_send,
    scatter_recv,
    gather_send,
    gather_recv,
):
    me = lax.axis_index("seq")
    chan = lax.axis_index("chan")
    sources = (
        (key, query, cotangent, tokens)
        + (first, second, feats, embed_table, short_conv, decay_rate, weight_third)
        + (skip_gain, twiddles, tables)
    )
    loads = [
        pltpu.make_async_copy(source, target, input_sems.at[n])
        for n, (source, target) in enumerate(zip(sources, held_inputs))
    ]
    for load in loads:
        load.start()
    key, query, cotangent, tokens, first, second, feats = held_inputs[:7]
    embed_table, short_conv, decay_rate, weight_third = held_inputs[7:11]
    skip_gain, twiddles, tables = held_inputs[11:]
    rows = key.shape[0]
    lanes = staged.shape[2]
    vocab = embed_table.shape[0]
    units = second.shape[0]
    feat = first.shape[0]
    length = count * rows
    share = vocab // count
    peers = [lax.rem(me + step, count) for step in range(1, count)]
    sources = [lax.rem(me + count - step, count) for step in range(1, count)]
    across = [lax.rem(chan + step, groups) for step in range(1, groups)]
    greet([(peer, chan) for peer in peers] + [(me, group) for group in across])

    def post(source, target, send, recv, device):
        copy = pltpu.make_async_remote_copy(
            src_ref=source,
            dst_ref=target,
            send_sem=send,
            recv_sem=recv,
            device_id=device,
            device_id_type=MESH,
        )
        copy.start()
        return copy

    for load in loads[:4]:
        load.wait()
    token_rows[...] = jnp.zeros_like(token_rows)
    token_rows[: tokens.shape[0]] = tokens[...].astype(f32)
    for number in range(count):
        pack_rows(number, query, key, cotangent, staged)
    pl.semaphore_wait(pltpu.get_barrier_semaphore(), len(peers) + len(across))
    token_copies = [
        post(token_rows, token_landed.at[me], token_send.at[n], token_recv.at[n], (peer, chan))
        for n, peer in enumerate(peers)
    ]
    out_copies = [
        post(staged.at[peer], arrived.at[me], out_send.at[n], out_recv.at[n], (peer, chan))
        for n, peer in enumerate(peers)
    ]
    arrived[me] = staged[me]
    token_landed[me] = token_rows[...]

    for load in loads[4:]:
        load.wait()
    table_high[...], table_low[...] = split(tables[...])

    columns = pl.ds(pl.multiple_of(me // 2 * lanes, lanes), lanes)
    parity = lax.rem(me, 2)

    def mine(array):
        lane = lax.broadcasted_iota(jnp.int32, array.shape, 1)
        return jnp.where(lane // (lanes // 2) == parity, array, swap(array))

    third = mine(weight_third[:, columns])
    table = mine(embed_table[:, columns].astype(f32)).astype(bf16)
    rate = mine(jnp.broadcast_to(decay_rate[:, columns], (8, lanes)))[:1]
    skip = mine(jnp.broadcast_to(skip_gain[:, columns], (8, lanes)))[:1]
    all_taps = [mine(jnp.broadcast_to(short_conv[j : j + 1, columns], (8, lanes))) for j in range(3)]
    taps = [tap[:1] for tap in all_taps]
    scale = jnp.sqrt(one_less_exp(2.0 * rate) / one_less_exp(2.0 * length * rate))
    low = low_lanes((rows, lanes))
    sign = jnp.where(low, 1.0, -1.0).astype(f32)

    pre_one = dot_full(first[...], feats[:feat], ((0,), (0,)))
    act_one = jnp.sin(pre_one)
    acts[0] = act_one
    acts[1] = jnp.cos(pre_one)
    pre_two = dot_full(second[...], act_one, ((0,), (0,)))
    acts[2] = jnp.sin(pre_two)
    acts[3] = jnp.cos(pre_two)
    row_ids = lax.broadcasted_iota(jnp.int32, (rows, lanes), 0).astype(f32)
    for block in range(count):
        act_rows = acts[2, :, block * rows : (block + 1) * rows].T
        window = scale * jnp.exp(-rate * (row_ids + float(block * rows)))
        windows[block] = window
        filters[block] = dot_full(act_rows, third) * window

    def spread(both):
        high, rest = split(both)
        product = (
            dot(table_high[...], high) + dot(table_high[...], rest) + dot(table_low[...], high)
        )
        return product[:rows], product[rows:]

    def turn_forward(real, imag, lane):
        cos_t = twiddles[lane, 0]
        sin_t = twiddles[lane, 1]
        by_cos, by_sin = spread(
            jnp.concatenate([real * cos_t + imag * sin_t, imag * cos_t - real * sin_t], axis=1)
        )
        return (
            by_cos[:, :lanes] + by_sin[:, lanes:],
            by_cos[:, lanes:] - by_sin[:, :lanes],
        )

    def forward(ref, lane):
        cos_sums, sin_sums = [], []
        for start in range(2):
            cos_sum = jnp.zeros((rows, lanes), f32)
            sin_sum = jnp.zeros((rows, lanes), f32)
            for n in range(start, count, 2):
                piece = ref[n]
                cos_sum = cos_sum + coefs[lane, n] * piece
                sin_sum = sin_sum + coefs[lane, count + n] * piece
            cos_sums.append(cos_sum)
            sin_sums.append(sin_sum)
        return (
            turn_forward(cos_sums[0] + cos_sums[1], -(sin_sums[0] + sin_sums[1]), lane),
            turn_forward(cos_sums[0] - cos_sums[1], sin_sums[0] - sin_sums[1], count - lane),
        )

    def add_back(ref, lane, near, far):
        (near_cos, near_sin), (far_cos, far_sin) = near, far
        by_parity = (
            (near_cos + far_cos, near_sin - far_sin),
            (near_cos - far_cos, near_sin + far_sin),
        )
        for n in range(count):
            cos_part, sin_part = by_parity[n % 2]
            ref[n] += (
                coefs[lane, 2 * count + n] * cos_part - coefs[lane, 3 * count + n] * sin_part
            )

    def transform_filter(lane, carry):
        for place, (real, imag) in zip((lane, count - lane), forward(filters, lane)):
            filter_spec[place, 0] = real
            filter_spec[place, 1] = imag * sign
        return carry

    lax.fori_loop(0, count // 2 + 1, transform_filter, 0)

    for copy in token_copies:
        copy.wait()
    embedded[:8] = jnp.zeros((8, lanes), f32)
    vocab_ids = lax.broadcasted_iota(jnp.int32, (vocab, lanes), 0).astype(f32)
    for block in range(count):
        for piece in range(rows // lanes):
            ids = token_landed[block, piece : piece + 1]
            matches = jnp.where(vocab_ids == ids, 1.0, 0.0)
            start = block * rows + piece * lanes
            onehot[:, start : start + lanes] = matches.astype(bf16)
            embedded[8 + start : 8 + start + lanes] = dot(matches.T.astype(bf16), table)
    for block in range(count):
        start = 8 + block * rows
        value[block] = (
            taps[0] * embedded[start : start + rows]
            + taps[1] * embedded[start - 1 : start - 1 + rows]
            + taps[2] * embedded[start - 2 : start - 2 + rows]
        )
    total[...] = jnp.zeros_like(total)
    shape_total[...] = jnp.zeros_like(shape_total)

    def gate(block):
        packed = arrived[block]
        state[block] = jnp.where(low, packed * value[block], packed)

    gate(me)
    for copy, source in zip(out_copies, sources):
        copy.wait()
        gate(source)

    def multiply(place, xr, xi):
        fr = filter_spec[place, 0]
        fi = filter_spec[place, 1]
        by_cos, by_sin = spread(jnp.concatenate([xr * fr - xi * fi, xr * fi + xi * fr], axis=1))
        zr = by_cos[:, :lanes] - by_sin[:, lanes:]
        zi = by_cos[:, lanes:] + by_sin[:, :lanes]
        cos_t = twiddles[place, 0]
        sin_t = twiddles[place, 1]
        gr, gi = swap(xr), swap(xi)
        shape_spec[place] = jnp.where(low, xr * gr + xi * gi, swap(xr * gi - xi * gr))
        return zr * cos_t - zi * sin_t, zr * sin_t + zi * cos_t

    def convolve(lane, carry):
        near, far = forward(state, lane)
        add_back(total, lane, multiply(lane, *near), multiply(count - lane, *far))
        return carry

    lax.fori_loop(0, count // 2 + 1, convolve, 0)

    def finish(block):
        summed_rows = total[block] + skip * state[block]
        total[block] = summed_rows
        return jnp.where(low, summed_rows, summed_rows * value[block])

    middle = rows // 2

    def post_back(n, part):
        places = pl.ds(part * middle, middle)
        return post(
            pay.at[peers[n], places],
            landed.at[me, places],
            back_send.at[part, n],
            back_recv.at[part, n],
            (peers[n], chan),
        )

    back_copies = []
    for n, peer in enumerate(peers):
        pay[peer] = finish(peer)
        back_copies.append(post_back(n, 0))
    landed[me] = finish(me)

    def correlate_one(place):
        cos_t = twiddles[place, 0]
        sin_t = twiddles[place, 1]
        by_cos, by_sin = spread(shape_spec[place])
        both = by_cos - sign * swap(by_sin)
        return both * jnp.where(low, cos_t, -sin_t), both * jnp.where(low, sin_t, cos_t)

    def correlate(lane, carry):
        add_back(shape_total, lane, correlate_one(lane), correlate_one(count - lane))
        return carry

    lax.fori_loop(0, count // 2 + 1, correlate, 0)
    inv_root = 1.0 / math.sqrt(length)
    third_sum = jnp.zeros((units, lanes), f32)
    third_low = jnp.where(low_lanes(third.shape), third, 0.0)
    for block in range(count):
        grad_rows = shape_total[block]
        grad_rows = (grad_rows + swap(grad_rows)) * windows[block]
        places = slice(block * rows, (block + 1) * rows)
        third_sum += dot_full(acts[2, :, places], grad_rows)
        acts[3, :, places] = dot_full(third_low, grad_rows, ((1,), (1,))) * acts[3, :, places]
    grad_pre_two = acts[3]
    grad_pre_one = dot_full(second[...], grad_pre_two) * acts[1]
    grad_both = jnp.concatenate([grad_pre_two, grad_pre_one], axis=0)
    from_act = dot_full(acts[0], grad_both, ((1,), (1,)))
    from_feats = dot_full(feats[...], grad_both, ((1,), (1,)))
    hidden = jnp.where(low_lanes(from_act.shape), from_act, from_feats) * inv_root
    strip = units // count
    for n in range(count):
        by_chan[chan, n] = hidden[n * strip : (n + 1) * strip]
    chan_copies = [
        post(by_chan.at[chan], by_chan.at[chan], chan_send.at[n], chan_recv.at[n], (me, group))
        for n, group in enumerate(across)
    ]

    for copy in chan_copies:
        copy.wait()
    for n in range(count):
        strip_sum = by_chan[0, n]
        for group in range(1, groups):
            strip_sum = strip_sum + by_chan[group, n]
        held[n] = strip_sum
    scatter_copies = [
        post(held.at[peer], by_seq.at[me], scatter_send.at[n], scatter_recv.at[n], (peer, chan))
        for n, peer in enumerate(peers)
    ]
    by_seq[me] = held[me]
    back_copies += [post_back(n, 1) for n in range(count - 1)]

    gated[length:] = jnp.zeros((8, lanes), f32)
    short_sums = [jnp.zeros((1, lanes), f32) for _ in range(3)]
    skip_sum = jnp.zeros((1, lanes), f32)
    for block in range(count):
        start = block * rows
        grad_value = total[block] * swap(arrived[block])
        gated[start : start + rows] = grad_value
        for j in range(3):
            short_sums[j] += jnp.sum(
                grad_value * embedded[8 + start - j : 8 + start - j + rows], axis=0, keepdims=True
            )
        skip_sum += jnp.sum(state[block] * swap(state[block]), axis=0, keepdims=True)
    embed_sum = jnp.zeros((vocab, lanes), f32)
    for block in range(count):
        start = block * rows
        high, rest = split(
            taps[0] * gated[start : start + rows]
            + taps[1] * gated[start + 1 : start + 1 + rows]
            + taps[2] * gated[start + 2 : start + 2 + rows]
        )
        matches = onehot[:, start : start + rows]
        embed_sum += dot(matches, high) + dot(matches, rest)
    half = units // 2
    fold = jnp.where(low_lanes((half, lanes)), third_sum[:half], third_sum[half:])
    sums = jnp.concatenate([fold, *short_sums, skip_sum, jnp.zeros((4, lanes), f32)], axis=0)
    for block in range(count):
        top = embed_sum[block * share : block * share + share // 2]
        bottom = embed_sum[block * share + share // 2 : (block + 1) * share]
        folded = jnp.where(low_lanes(top.shape), swap(top), bottom)
        small[block] = jnp.concatenate([folded, sums], axis=0) * inv_root
    small_copies = [
        post(small.at[peer], small_landed.at[me], small_send.at[n], small_recv.at[n], (peer, chan))
        for n, peer in enumerate(peers)
    ]
    small_landed[me] = small[me]

    for copy in scatter_copies:
        copy.wait()
    strip_sum = by_seq[0]
    for n in range(1, count):
        strip_sum = strip_sum + by_seq[n]
    summed[me] = strip_sum
    gather_copies = [
        post(summed.at[me], summed.at[me], gather_send.at[n], gather_recv.at[n], (peer, chan))
        for n, peer in enumerate(peers)
    ]
    for copy in back_copies + small_copies + gather_copies:
        copy.wait()


def finish_kernel(
    landed,
    small_landed,
    summed,
    query,
    cotangent,
    out,
    grad_query,
    grad_key,
    grad_embed,
    grad_short,
    grad_skip,
    grad_first,
    grad_second,
    grad_third,
):
    count, rows, lanes = landed.shape
    low = low_lanes((rows, lanes))
    share = grad_embed.shape[0]
    part = share // 2
    half = grad_third.shape[0] // 2
    for block in range(count // 2):
        columns = slice(block * lanes, (block + 1) * lanes)
        even, odd = landed[2 * block], landed[2 * block + 1]
        inner = jnp.where(low, even, swap(odd))
        out[:, columns] = (query[:, columns].astype(f32) * inner).astype(bf16)
        grad_query[:, columns] = (cotangent[:, columns].astype(f32) * inner).astype(bf16)
        grad_key[:, columns] = jnp.where(low, swap(even), odd).astype(bf16)
        even, odd = small_landed[2 * block], small_landed[2 * block + 1]
        left = low_lanes(even.shape)
        first_rows = jnp.where(left, even, swap(odd))
        last_rows = jnp.where(left, swap(even), odd)
        grad_embed[:part, columns] = first_rows[:part]
        grad_embed[part:, columns] = last_rows[:part]
        grad_third[:half, columns] = first_rows[part : part + half]
        grad_third[half:, columns] = last_rows[part : part + half]
        top = part + half
        grad_short[:, columns] = last_rows[top : top + 3]
        grad_skip[:, columns] = last_rows[top + 3 : top + 4]
    both = jnp.concatenate([summed[n] for n in range(count)], axis=0)
    units = grad_second.shape[0]
    grad_second[...] = both[:, :units]
    grad_first[...] = swap(both)[: grad_first.shape[0], :units]


def feature_table(length):
    positions = np.arange(length, dtype=np.int64)
    frequency = 2 ** np.arange(BANDS, dtype=np.int64) + 1
    phases = positions[:, None] * frequency[None, :] % length
    angles = phases.astype(np.float32) * np.float32(two_pi / length)
    ramp = positions.astype(np.float32)[:, None] / np.float32(length)
    return np.concatenate([ramp, np.cos(angles), np.sin(angles)], axis=1).T.astype(np.float32)


def fused_device(
    tokens,
    embed_table,
    short_conv,
    query_branch,
    key_branch,
    decay_rate,
    weight_first,
    weight_second,
    weight_third,
    skip_gain,
    cotangent,
):
    count = lax.axis_size("seq")
    groups = lax.axis_size("chan")
    seq_index = lax.axis_index("seq")
    rows, chan_width = query_branch.shape
    length = rows * count
    points = 2 * length
    vocab = embed_table.shape[0]
    hidden_units = weight_second.shape[0]
    feat = weight_first.shape[0]
    slice_width = chan_width // count
    lanes = 2 * slice_width
    share = vocab // count
    strip = hidden_units // count
    small_rows = share // 2 + hidden_units // 2 + 8
    vmem = pl.BlockSpec(memory_space=pltpu.VMEM)
    smem = pl.BlockSpec(memory_space=pltpu.SMEM)
    dma = pltpu.SemaphoreType.DMA

    depth = np.arange(rows)
    turns = np.arange(count + 1)
    angle = two_pi * (depth[:, None] * depth[None, :] % rows) / rows
    tables = np.concatenate([np.cos(angle), np.sin(angle)], axis=0).astype(np.float32)
    twist = two_pi * (turns[:, None] * depth[None, :]) / points
    twiddles = np.stack([np.cos(twist), np.sin(twist)], axis=1).astype(np.float32)
    twiddles = np.broadcast_to(twiddles[..., None], (count + 1, 2, rows, lanes)).copy()
    small_angle = two_pi * (turns[:, None] * np.arange(count)[None, :] % (2 * count)) / (2 * count)
    weight = np.where(turns % (count // 2) == 0, 1.0, 2.0)[:, None] / points
    coefs = np.concatenate(
        [
            np.cos(small_angle),
            np.sin(small_angle),
            weight * np.cos(small_angle),
            weight * np.sin(small_angle),
        ],
        axis=1,
    ).astype(np.float32)
    feats = np.pad(feature_table(length), ((0, hidden_units - feat), (0, 0)))

    def whole(*shape):
        return jax.ShapeDtypeStruct(shape, f32)

    def buffer(*shape):
        return pltpu.VMEM(shape, f32)

    block_shape = (count, rows, lanes)
    operands = (
        tokens.reshape(rows // lanes, lanes),
        embed_table,
        short_conv,
        query_branch,
        key_branch,
        cotangent,
        decay_rate[None],
        weight_first,
        weight_second,
        weight_third,
        skip_gain[None],
        jnp.asarray(feats),
        jnp.asarray(twiddles),
        jnp.asarray(tables),
    )
    load_order = (4, 3, 5, 0, 7, 8, 11, 1, 2, 6, 9, 10, 12, 13)
    landed, small_landed, summed = pl.pallas_call(
        functools.partial(fused_kernel, count, groups),
        out_shape=(
            whole(*block_shape),
            whole(count, small_rows, lanes),
            whole(count, strip, lanes),
        ),
        in_specs=[smem] + [pl.BlockSpec(memory_space=pltpu.HBM)] * 14,
        out_specs=(vmem,) * 3,
        scratch_shapes=[
            [pltpu.VMEM(operands[n].shape, operands[n].dtype) for n in load_order],
            dma((len(load_order),)),
            pltpu.VMEM(tables.shape, bf16),
            pltpu.VMEM(tables.shape, bf16),
            buffer(*block_shape),
            buffer(*block_shape),
            buffer(8, lanes),
            buffer(count, 8, lanes),
            buffer(*block_shape),
            buffer(*block_shape),
            buffer(*block_shape),
            buffer(*block_shape),
            buffer(*block_shape),
            buffer(*block_shape),
            buffer(length + 8, lanes),
            buffer(length + 8, lanes),
            pltpu.VMEM((vocab, length), bf16),
            buffer(4, hidden_units, length),
            buffer(count + 1, 2, rows, lanes),
            buffer(count + 1, rows, lanes),
            buffer(*block_shape),
            buffer(count, small_rows, lanes),
            buffer(groups, count, strip, lanes),
            buffer(count, strip, lanes),
            buffer(count, strip, lanes),
        ]
        + [dma((count,))] * 4
        + [dma((2, count))] * 2
        + [dma((count,))] * 2
        + [dma((groups,))] * 2
        + [dma((count,))] * 4,
        compiler_params=pltpu.CompilerParams(
            collective_id=0, has_side_effects=True, vmem_limit_bytes=56 * 2**20
        ),
        name="convolve_slices",
    )(jnp.asarray(coefs), *operands)
    half_out = jax.ShapeDtypeStruct((rows, chan_width), bf16)
    results = pl.pallas_call(
        finish_kernel,
        out_shape=(
            half_out,
            half_out,
            half_out,
            whole(share, chan_width),
            whole(3, chan_width),
            whole(1, chan_width),
            whole(feat, hidden_units),
            whole(hidden_units, hidden_units),
            whole(hidden_units, chan_width),
        ),
        in_specs=[vmem] * 5,
        out_specs=(vmem,) * 9,
        compiler_params=pltpu.CompilerParams(vmem_limit_bytes=60 * 2**20),
        name="finish_outputs",
    )(landed, small_landed, summed, query_branch, cotangent)
    return results[:5] + (results[5][0],) + results[6:]


def per_slice(*arrays):
    count = lax.axis_size("seq")
    rows, width = arrays[3].shape
    lanes = 2 * width // count
    units = arrays[7].shape[0]
    vocab = arrays[1].shape[0]
    tiled = lanes % 128 == 0 and rows % lanes == 0 and rows <= 8 * lanes
    even = count % 2 == 0 and 2 * units == lanes and units % (8 * count) == 0
    body = fused_device if tiled and even and vocab % (16 * count) == 0 else per_device
    return body(*arrays)


def solution(mesh):
    in_specs = (
        P("seq"),
        P(None, "chan"),
        P(None, "chan"),
        P("seq", "chan"),
        P("seq", "chan"),
        P("chan"),
        P(),
        P(),
        P(None, "chan"),
        P("chan"),
        P("seq", "chan"),
    )
    out_specs = (
        P("seq", "chan"),
        P("seq", "chan"),
        P("seq", "chan"),
        P("seq", "chan"),
        P(None, "chan"),
        P("chan"),
        P(),
        P(),
        P(None, "chan"),
    )
    return jax.shard_map(
        per_slice, mesh=mesh, in_specs=in_specs, out_specs=out_specs, check_vma=False
    )
```
